32 devices in a mesh: lon: 8 (over z, core), lat: 4 (over y, x).
Axes of the slice: x: 2, y: 2, z: 4, core: 2. Of those that a mesh axis runs over, the one named last changes fastest.
Arguments:
- innovations: bfloat16 [7, 1024, 16, 128], P(None, ('lon', 'lat')), may hold values from -6 to 6
- fractions: bfloat16 [7, 1024, 2, 128], P(None, ('lon', 'lat')), may hold values from 0 to 1
- cell_index: int32 [7, 1024, 128], P(None, ('lon', 'lat')), may hold values from 0 to 238, as said below
- counts: int32 [7, 1024, 2], P(None, ('lon', 'lat')), may hold values from 0 to 64, as said below
- blocks: int32 [7, 1024, 2], P(None, ('lon', 'lat')), may hold values from 0 to 15
- u_wind: float32 [4, 128, 1024], P(None, 'lat', 'lon'), may hold values from -0.5 to 0.5
- v_wind: float32 [4, 128, 1024], P(None, 'lat', 'lon'), may hold values from -0.5 to 0.5
- channel_mix: float32 [16, 16], replicated
Outputs:
- gradient: float32 [4, 4, 128, 1024], P(None, None, 'lat', 'lon')
The draws below stay inside these ranges and needn't reach their ends.
Inputs may be any that keep to these rules, and one draw needn't show every extreme that they name: Row and column of a cell inside its tile, cell_index // 16 and cell_index % 16, are each at most 14. `counts`: in every draw some receiving device gets 64 live observations in every tile from every sender.
All inputs are finite; a program needn't handle non-finite values.
Results may differ from the reference program's by a relative error of at most 0.0003.
Values may be sent and summed in bfloat16 or wider, within the bound.
A program may use at most 192 MiB of HBM per device.

```python
import math
import jax
import jax.numpy as jnp
from jax import lax

VARS = 4
LEV = 4
CH = 16
TILE = 16
J = 64
CAP = 2
SLOTS = 7
CLAT = 32
CLON = 128
NLAT = 128
NLON = 1024
BLOCKS_DEV = 16
N_LAT = 4
DEVICES = 32


def draw_cell_index(key, part):
    first, second, third = jax.random.split(key, 3)
    shape = (SLOTS, DEVICES * DEVICES, CAP * J)
    row_part = jax.random.randint(first, shape, 0, TILE - 1)
    col_part = jax.random.randint(second, shape, 0, TILE - 1)
    cell_all = (row_part * TILE + col_part).reshape(-1)
    where_top = jax.random.randint(third, (), 0, cell_all.shape[0])
    cell_all = cell_all.at[where_top].set(TILE * TILE - TILE - 2)
    return cell_all.reshape(shape).astype(jnp.int32)


def draw_counts(key, part):
    first, second, third = jax.random.split(key, 3)
    shape = (SLOTS, DEVICES * DEVICES, CAP)
    base_count = jax.random.randint(first, shape, 0, J + 1)
    dense_dest = jax.random.randint(second, (DEVICES,), 0, 4) == 0
    chosen = jax.random.randint(third, (), 0, DEVICES)
    dense_dest = dense_dest.at[chosen].set(True)
    dense_pair = jnp.tile(dense_dest, DEVICES)[None, :, None]
    return jnp.where(dense_pair, J, base_count // 2).astype(jnp.int32)


def draw_channel_mix(key, part):
    first, second = jax.random.split(key, 2)
    diagonal = jax.random.uniform(first, (CH,), jnp.float32, 0.5, 1.0)
    off_part = 0.25 / math.sqrt(CH) * jax.random.normal(second, (CH, CH), jnp.float32)
    return (off_part + jnp.eye(CH, dtype=jnp.float32) * diagonal[None, :]).astype(jnp.float32)


def with_ends(values, key, smallest, high):
    shape = values.shape
    spot = [jax.random.randint(jax.random.fold_in(key, axis), (), 0, shape[axis]) for axis in range(len(shape))]
    values = values.at[tuple(spot)].set(smallest)
    longest = shape.index(max(shape))
    spot[longest] = (spot[longest] + 1) % shape[longest]
    return values.at[tuple(spot)].set(high)


def level_of(own_key, dims, pieces, low, high):
    def one(position, shards_of):
        steps = jax.random.uniform(jax.random.fold_in(jax.random.fold_in(own_key, 6), position), (shards_of,), jnp.float32, low / len(pieces), high / len(pieces))
        return jnp.repeat(jnp.exp(steps), dims[position] // shards_of).reshape((-1,) + (1,) * (len(dims) - position - 1))

    loudness = one(*pieces[0])
    for cut in pieces[1:]:
        loudness = loudness * one(*cut)
    return loudness


def scatter_about(rng, dims, scale, most, cuts=(), kind=jnp.bfloat16):
    result = jax.random.normal(rng, dims, jnp.float32) * scale
    if len(cuts) > 0:
        result = level_of(rng, dims, cuts, -0.22, 0.18) * result
    return jnp.clip(result, min=-most, max=most).astype(kind)


def setup_inputs(seed: int = 0) -> dict:
    keys = jax.random.split(jax.random.key(seed), 9)
    return {
        "innovations": scatter_about(keys[0], (SLOTS, DEVICES * DEVICES, CH, CAP * J), 1.0, 6.0, ((1, 32),)),
        "fractions": jnp.clip(1.0 * jax.random.uniform(keys[1], (SLOTS, DEVICES * DEVICES, 2, CAP * J), jnp.float32) ** level_of(keys[1], (SLOTS, DEVICES * DEVICES, 2, CAP * J), ((1, 32),), -0.2, 0.2), 0.0, 1.0).astype(jnp.bfloat16),
        "cell_index": draw_cell_index(jax.random.fold_in(keys[8], 71), 0),
        "counts": draw_counts(jax.random.fold_in(keys[8], 71), 0),
        "blocks": with_ends(jax.random.randint(keys[4], (SLOTS, DEVICES * DEVICES, CAP), 0, BLOCKS_DEV), jax.random.fold_in(keys[4], 1), 0, BLOCKS_DEV - 1).astype(jnp.int32),
        "u_wind": jnp.clip(jax.random.uniform(keys[5], (LEV, NLAT, NLON), jnp.float32, -0.5, 0.5) * level_of(keys[5], (LEV, NLAT, NLON), ((1, 4), (2, 8)), -0.4, 0.0), -0.5, 0.5),
        "v_wind": jnp.clip(jax.random.uniform(keys[6], (LEV, NLAT, NLON), jnp.float32, -0.5, 0.5) * level_of(keys[6], (LEV, NLAT, NLON), ((1, 4), (2, 8)), -0.4, 0.0), -0.5, 0.5),
        "channel_mix": draw_channel_mix(jax.random.fold_in(keys[8], 71), 0),
    }


KAPPA = 0.125
HIGHEST = lax.Precision.HIGHEST


def lat_next(layer_stack):
    return jnp.pad(layer_stack, ((0, 0), (0, 0), (0, 1), (0, 0)))[:, :, 1:, :]


def lat_prev(layer_stack):
    return jnp.pad(layer_stack, ((0, 0), (0, 0), (1, 0), (0, 0)))[:, :, :-1, :]


def adjoint_op(adjoint_field, u_wind, v_wind, channel_mix):
    mixed = jnp.einsum('dc,dn->cn', channel_mix, adjoint_field.reshape(CH, NLAT * NLON), precision=HIGHEST)
    mixed = mixed.reshape(VARS, LEV, NLAT, NLON)
    east_flux = u_wind[None] * mixed
    north_flux = v_wind[None] * mixed
    spread = jnp.roll(mixed, -1, 3) + jnp.roll(mixed, 1, 3) + lat_next(mixed) + lat_prev(mixed)
    carry_term = 0.5 * (jnp.roll(east_flux, -1, 3) - jnp.roll(east_flux, 1, 3)) + 0.5 * (lat_next(north_flux) - lat_prev(north_flux))
    return (1.0 - 4.0 * KAPPA) * mixed + KAPPA * spread + carry_term


def slot_forcing(innov_slot, frac_slot, cell_slot, count_slot, block_slot):
    pairs = DEVICES * DEVICES
    width = CAP * J
    slot_pos = jnp.arange(width, dtype=jnp.int32)
    tile_of = slot_pos // J
    count_each = count_slot[:, tile_of]
    is_live = (slot_pos % J)[None, :] < count_each
    block_each = block_slot[:, tile_of]
    target = jnp.arange(pairs, dtype=jnp.int32) % DEVICES
    lon_index = target // N_LAT
    lat_index = target % N_LAT
    across = CLON // TILE
    row_base = (lat_index * CLAT)[:, None] + (block_each // across) * TILE + cell_slot // TILE
    col_base = (lon_index * CLON)[:, None] + (block_each % across) * TILE + cell_slot % TILE
    frac_y = frac_slot[:, 0, :].astype(jnp.float32)
    frac_x = frac_slot[:, 1, :].astype(jnp.float32)
    live_mask = jnp.where(is_live, 1.0, 0.0).astype(jnp.float32)
    values = jnp.transpose(innov_slot.astype(jnp.float32), (0, 2, 1))
    grid_sum = jnp.zeros((NLAT * NLON, CH), jnp.float32)
    corners = ((0, 0, (1.0 - frac_y) * (1.0 - frac_x)), (0, 1, (1.0 - frac_y) * frac_x),
               (1, 0, frac_y * (1.0 - frac_x)), (1, 1, frac_y * frac_x))
    for shift_y, shift_x, weight in corners:
        flat_index = ((row_base + shift_y) * NLON + col_base + shift_x).reshape(-1).astype(jnp.int32)
        update = (values * (weight * live_mask)[:, :, None]).reshape(-1, CH)
        grid_sum = grid_sum.at[flat_index].add(update)
    return jnp.transpose(grid_sum.reshape(NLAT, NLON, VARS, LEV), (2, 3, 0, 1))


def reference(innovations, fractions, cell_index, counts, blocks, u_wind, v_wind, channel_mix):
    forcing = [slot_forcing(innovations[slot], fractions[slot], cell_index[slot], counts[slot], blocks[slot])
               for slot in range(SLOTS)]
    adjoint_field = forcing[SLOTS - 1]
    for later in range(SLOTS - 2, -1, -1):
        adjoint_field = adjoint_op(adjoint_field, u_wind, v_wind, channel_mix) + forcing[later]
    return adjoint_field
```

```python
import functools

import jax
import jax.numpy as jnp
from jax import lax
from jax.experimental import pallas as pl
from jax.experimental.pallas import tpu as pltpu
from jax.sharding import PartitionSpec as P

VARS = 4
LEV = 4
CH = 16
TILE = 16
KAPPA = 0.125
EDGE = 8
GROUP = 4
MESH = pl.DeviceIdType.MESH


def kernel(
    n_lon, n_lat, slots, lat_cells, lon_cells,
    mix_ref, innov_ref, meta_ref, u_ref, v_ref, out_ref,
    got_innov, got_meta, rows_buf, acc, field, mixed, wind, wind_send, wind_got, lon_send, lon_got,
    own_sem, innov_send, innov_recv, meta_send, meta_recv,
    wlat_send, wlat_recv, wlon_send, wlon_recv, flat_send, flat_recv, flon_send, flon_recv,
):
    devices = n_lon * n_lat
    my_lon, my_lat = lax.axis_index("lon"), lax.axis_index("lat")
    me = my_lon * n_lat + my_lat
    width = got_innov.shape[-1]
    span = GROUP * width
    tall = lat_cells + 2 * EDGE
    low, high = EDGE, EDGE + lat_cells

    lat_up = (my_lon, (my_lat + 1) % n_lat)
    lat_down = (my_lon, (my_lat + n_lat - 1) % n_lat)
    lon_up = ((my_lon + 1) % n_lon, my_lat)
    lon_down = ((my_lon + n_lon - 1) % n_lon, my_lat)

    barrier = pltpu.get_barrier_semaphore()

    @pl.loop(1, devices)
    def _(k):
        to = (me + k) % devices
        pl.semaphore_signal(barrier, inc=1, device_id=(to // n_lat, to % n_lat), device_id_type=MESH)

    own_a = pltpu.make_async_copy(innov_ref.at[:, me], got_innov.at[0], own_sem.at[0])
    own_b = pltpu.make_async_copy(meta_ref.at[me], got_meta.at[0], own_sem.at[1])
    own_a.start()
    own_b.start()
    wind[0:LEV, low:high, 0:lon_cells] = u_ref[...]
    wind[LEV : 2 * LEV, low:high, 0:lon_cells] = v_ref[...]
    pl.semaphore_wait(barrier, devices - 1)

    def lat_pair(buffer, send, recv):
        down = pltpu.make_async_remote_copy(
            src_ref=buffer.at[:, low : low + EDGE, 0:lon_cells],
            dst_ref=buffer.at[:, high : high + EDGE, 0:lon_cells],
            send_sem=send.at[0], recv_sem=recv.at[0], device_id=lat_down, device_id_type=MESH,
        )
        up = pltpu.make_async_remote_copy(
            src_ref=buffer.at[:, high - EDGE : high, 0:lon_cells],
            dst_ref=buffer.at[:, 0:low, 0:lon_cells],
            send_sem=send.at[1], recv_sem=recv.at[1], device_id=lat_up, device_id_type=MESH,
        )
        return down, up

    def lon_pair(send_buf, got_buf, send, recv):
        down = pltpu.make_async_remote_copy(
            src_ref=send_buf.at[0], dst_ref=got_buf.at[0],
            send_sem=send.at[0], recv_sem=recv.at[0], device_id=lon_down, device_id_type=MESH,
        )
        up = pltpu.make_async_remote_copy(
            src_ref=send_buf.at[1], dst_ref=got_buf.at[1],
            send_sem=send.at[1], recv_sem=recv.at[1], device_id=lon_up, device_id_type=MESH,
        )
        return down, up

    lane = lax.broadcasted_iota(jnp.int32, (tall, lon_cells), 1)

    def pack(source, count, target):
        first = jnp.zeros((tall, lon_cells), jnp.float32)
        last = first
        for c in range(count):
            body = source[c, :, 0:lon_cells]
            here = (lane >= EDGE * c) & (lane < EDGE * (c + 1))
            a = body if c == 0 else pltpu.roll(body, EDGE * c, 1)
            shift = (EDGE * (c + 1)) % lon_cells
            b = body if shift == 0 else pltpu.roll(body, shift, 1)
            first = jnp.where(here, a, first)
            last = jnp.where(here, b, last)
        target[0] = first
        target[1] = last

    def unpack(got, count, target):
        after, before = got[0], got[1]
        for c in range(count):
            back = (lon_cells - EDGE * c) % lon_cells
            a = after if back == 0 else pltpu.roll(after, back, 1)
            shift = (lon_cells - EDGE - EDGE * c) % lon_cells
            b = before if shift == 0 else pltpu.roll(before, shift, 1)
            target[c, :, lon_cells : 2 * lon_cells] = jnp.where(lane < EDGE, a, b)

    wind_lat = lat_pair(wind, wlat_send, wlat_recv)
    for copy in wind_lat:
        copy.start()

    def exchange(k):
        to = (me + k) % devices
        where = (to // n_lat, to % n_lat)
        big = pltpu.make_async_remote_copy(
            src_ref=innov_ref.at[:, to], dst_ref=got_innov.at[k],
            send_sem=innov_send.at[k], recv_sem=innov_recv.at[k], device_id=where, device_id_type=MESH,
        )
        small = pltpu.make_async_remote_copy(
            src_ref=meta_ref.at[to], dst_ref=got_meta.at[k],
            send_sem=meta_send.at[k], recv_sem=meta_recv.at[k], device_id=where, device_id_type=MESH,
        )
        return small, big

    @pl.loop(1, devices)
    def _(k):
        for copy in exchange(k):
            copy.start()

    @pl.loop(0, slots)
    def _(s):
        acc[s] = jnp.zeros(acc.shape[1:], jnp.float32)

    own_a.wait()
    own_b.wait()
    for copy in wind_lat:
        copy.wait()
    pack(wind, 2 * LEV, wind_send)
    wind_lon = lon_pair(wind_send, wind_got, wlon_send, wlon_recv)
    for copy in wind_lon:
        copy.start()

    row_id = lax.broadcasted_iota(jnp.int32, (lat_cells, span), 0).astype(jnp.float32)
    col_id = lax.broadcasted_iota(jnp.int32, (lon_cells, span), 0).astype(jnp.float32)
    contract = (((1,), (1,)), ((), ()))

    @pl.loop(0, devices // GROUP)
    def _(g):
        for i in range(GROUP):
            k = g * GROUP + i

            @pl.when(k > 0)
            def _():
                for copy in exchange(k):
                    copy.wait_recv()

            numbers = got_meta[k].astype(jnp.float32)
            for s in range(slots):
                rows_buf[s, 0:4, i * width : (i + 1) * width] = numbers[4 * s : 4 * s + 4]

        @pl.loop(0, slots)
        def _(s):
            values = jnp.concatenate(
                [got_innov[g * GROUP + i, s] for i in range(GROUP)], axis=1
            ).astype(jnp.float32)
            frac_y, frac_x = rows_buf[s, 0:1], rows_buf[s, 1:2]
            row, col = rows_buf[s, 2:3], rows_buf[s, 3:4]
            at_row = jnp.where(row_id == row, 1.0, 0.0).astype(jnp.bfloat16)
            at_next = jnp.where(row_id == row + 1.0, 1.0, 0.0).astype(jnp.bfloat16)
            hit = col_id == col
            cols = jnp.concatenate(
                [jnp.where(hit, 1.0, 0.0).astype(jnp.bfloat16), jnp.where(hit, frac_x, 0.0).astype(jnp.bfloat16)], axis=0
            )
            lower = values * (1.0 - frac_y)
            upper = values * frac_y
            lower_hi = lower.astype(jnp.bfloat16).astype(jnp.float32)
            upper_hi = upper.astype(jnp.bfloat16).astype(jnp.float32)
            lower_lo = lower - lower_hi
            upper_lo = upper - upper_hi

            def spread(low_part, up_part):
                pieces = []
                for c in range(CH):
                    a = jnp.broadcast_to(low_part[c : c + 1], (16, span)).astype(jnp.bfloat16)
                    b = jnp.broadcast_to(up_part[c : c + 1], (16, span)).astype(jnp.bfloat16)
                    for r in range(0, lat_cells, 16):
                        pieces.append(a * at_row[r : r + 16] + b * at_next[r : r + 16])
                return jnp.concatenate(pieces, axis=0)

            total = lax.dot_general(
                spread(lower_hi, upper_hi), cols, contract, preferred_element_type=jnp.float32
            )
            total = total + lax.dot_general(
                spread(lower_lo, upper_lo), cols, contract, preferred_element_type=jnp.float32
            )
            acc[s] += total

    def settle(s):
        plain = acc[s, :, 0:lon_cells]
        part = acc[s, :, lon_cells : 2 * lon_cells]
        whole = plain - part + pltpu.roll(part, 1, 1)
        field[s, :, low:high, 0:lon_cells] = whole.reshape(CH, lat_cells, lon_cells)

    lat_copies = {}
    for s in range(slots - 1, -1, -1):
        settle(s)
        if s > 0:
            lat_copies[s] = lat_pair(field.at[s], flat_send.at[s], flat_recv.at[s])
            for copy in lat_copies[s]:
                copy.start()
    for copy in wind_lon:
        copy.wait()
    unpack(wind_got, 2 * LEV, wind)
    lon_copies = {}
    for s in range(slots - 1, 0, -1):
        for copy in lat_copies[s]:
            copy.wait()
        pack(field.at[s], CH, lon_send.at[s])
        lon_copies[s] = lon_pair(lon_send.at[s], lon_got.at[s], flon_send.at[s], flon_recv.at[s])
        for copy in lon_copies[s]:
            copy.start()

    row_at = lax.broadcasted_iota(jnp.int32, (tall, 2 * lon_cells), 0)
    first = jnp.where(my_lat == 0, low, 0)
    last = jnp.where(my_lat == n_lat - 1, high, tall)
    inside = (row_at >= first) & (row_at < last)

    for s in range(slots - 1, -1, -1):
        if s > 0:
            for copy in lon_copies[s]:
                copy.wait()
            unpack(lon_got.at[s], CH, field.at[s])
        if s == slots - 1:
            continue
        older = s + 1

        @pl.loop(0, CH)
        def _(c):
            total = mix_ref[0, c] * field[older, 0]
            for d in range(1, CH):
                total = total + mix_ref[d, c] * field[older, d]
            total = jnp.where(inside, total, 0.0)
            level = c % LEV
            eastward = (0.5 * wind[level]) * total
            northward = (0.5 * wind[LEV + level]) * total
            near = KAPPA * total
            result = (
                (1.0 - 4.0 * KAPPA) * total
                + pltpu.roll(near + eastward, 2 * lon_cells - 1, 1)
                + pltpu.roll(near - eastward, 1, 1)
                + pltpu.roll(near + northward, tall - 1, 0)
                + pltpu.roll(near - northward, 1, 0)
            )
            if s > 0:
                mixed[c] = result
            else:
                out_ref[c] = result[low:high, 0:lon_cells] + field[0, c, low:high, 0:lon_cells]

        if s > 0:

            @pl.loop(0, CH)
            def _(c):
                field[s, c] += mixed[c]

    @pl.loop(1, devices)
    def _(k):
        for copy in exchange(k):
            copy.wait_send()


def shards(n_lon, n_lat, innovations, fractions, cell_index, counts, blocks, u_wind, v_wind, channel_mix):
    slots, devices, channels, width = innovations.shape
    lat_cells, lon_cells = u_wind.shape[1:]
    across = lon_cells // TILE
    tiles = counts.shape[2]
    per_tile = width // tiles
    within = lax.broadcasted_iota(jnp.int32, (1, 1, tiles, per_tile), 3)
    live = within < counts[..., None]
    cell = cell_index.reshape(slots, devices, tiles, per_tile)
    block = blocks[..., None]
    row = jnp.where(live, (block // across) * TILE + cell // TILE, -100)
    col = (block % across) * TILE + cell % TILE
    places = jnp.stack([row, col], axis=2).reshape(slots, devices, 2, width).astype(jnp.bfloat16)
    meta = jnp.concatenate([fractions, places], axis=2)
    meta = jnp.transpose(meta, (1, 0, 2, 3)).reshape(devices, 4 * slots, width)
    meta_rows = -(-4 * slots // 16) * 16
    meta = jnp.pad(meta, ((0, 0), (0, meta_rows - 4 * slots), (0, 0)))

    tall, wide = lat_cells + 2 * EDGE, 2 * lon_cells
    f32, bf16, dma = jnp.float32, jnp.bfloat16, pltpu.SemaphoreType.DMA
    vmem = pl.BlockSpec(memory_space=pltpu.VMEM)
    out = pl.pallas_call(
        functools.partial(kernel, n_lon, n_lat, slots, lat_cells, lon_cells),
        out_shape=jax.ShapeDtypeStruct((CH, lat_cells, lon_cells), f32),
        in_specs=[
            pl.BlockSpec(memory_space=pltpu.SMEM),
            pl.BlockSpec(memory_space=pl.ANY),
            pl.BlockSpec(memory_space=pl.ANY),
            vmem,
            vmem,
        ],
        out_specs=vmem,
        scratch_shapes=[
            pltpu.VMEM((devices, slots, channels, width), bf16),
            pltpu.VMEM((devices, meta_rows, width), bf16),
            pltpu.VMEM((slots, 8, GROUP * width), f32),
            pltpu.VMEM((slots, CH * lat_cells, wide), f32),
            pltpu.VMEM((slots, CH, tall, wide), f32),
            pltpu.VMEM((CH, tall, wide), f32),
            pltpu.VMEM((2 * LEV, tall, wide), f32),
            pltpu.VMEM((2, tall, lon_cells), f32),
            pltpu.VMEM((2, tall, lon_cells), f32),
            pltpu.VMEM((slots, 2, tall, lon_cells), f32),
            pltpu.VMEM((slots, 2, tall, lon_cells), f32),
            dma((2,)),
            dma((devices,)),
            dma((devices,)),
            dma((devices,)),
            dma((devices,)),
            dma((2,)),
            dma((2,)),
            dma((2,)),
            dma((2,)),
            dma((slots, 2)),
            dma((slots, 2)),
            dma((slots, 2)),
            dma((slots, 2)),
        ],
        compiler_params=pltpu.CompilerParams(
            collective_id=0, has_side_effects=True, vmem_limit_bytes=48 * 1024 * 1024
        ),
    )(channel_mix, innovations, meta, u_wind, v_wind)
    return out.reshape(VARS, LEV, lat_cells, lon_cells)


def solution(mesh):
    in_specs = (
        P(None, ("lon", "lat"), None, None),
        P(None, ("lon", "lat"), None, None),
        P(None, ("lon", "lat"), None),
        P(None, ("lon", "lat"), None),
        P(None, ("lon", "lat"), None),
        P(None, "lat", "lon"),
        P(None, "lat", "lon"),
        P(),
    )
    out_specs = P(None, None, "lat", "lon")
    body = functools.partial(shards, mesh.shape["lon"], mesh.shape["lat"])
    return jax.shard_map(body, mesh=mesh, in_specs=in_specs, out_specs=out_specs, check_vma=False)
```

```python
import functools

import jax
import jax.numpy as jnp
from jax import lax
from jax.experimental import pallas as pl
from jax.experimental.pallas import tpu as pltpu
from jax.sharding import PartitionSpec as P

VARS = 4
LEV = 4
CH = 16
TILE = 16
KAPPA = 0.125
EDGE = 8
GROUP = 4
AHEAD = 2
MESH = pl.DeviceIdType.MESH


def kernel(
    n_lon, n_lat, slots, lat_cells, lon_cells,
    mix_ref, innov_ref, meta_ref, u_ref, v_ref, out_ref,
    got_innov, got_meta, rows_buf, acc, field, wind, wind_send, wind_got, lon_send, lon_got,
    own_sem, innov_send, innov_recv, meta_send, meta_recv,
    wlat_send, wlat_recv, wlon_send, wlon_recv, flat_send, flat_recv, flon_send, flon_recv,
):
    devices = n_lon * n_lat
    my_lon, my_lat = lax.axis_index("lon"), lax.axis_index("lat")
    me = my_lon * n_lat + my_lat
    width = got_innov.shape[-1]
    span = GROUP * width
    tall = lat_cells + 2 * EDGE
    low, high = EDGE, EDGE + lat_cells
    metas = got_meta.shape[0]

    lat_up = (my_lon, (my_lat + 1) % n_lat)
    lat_down = (my_lon, (my_lat + n_lat - 1) % n_lat)
    lon_up = ((my_lon + 1) % n_lon, my_lat)
    lon_down = ((my_lon + n_lon - 1) % n_lon, my_lat)

    barrier = pltpu.get_barrier_semaphore()

    @pl.loop(1, devices)
    def _(k):
        to = (me + k) % devices
        pl.semaphore_signal(barrier, inc=1, device_id=(to // n_lat, to % n_lat), device_id_type=MESH)

    own_a = pltpu.make_async_copy(innov_ref.at[:, me], got_innov.at[:, 0], own_sem.at[0])
    own_b = pltpu.make_async_copy(meta_ref.at[:, me], got_meta.at[:, 0], own_sem.at[1])
    own_a.start()
    own_b.start()
    wind[0:LEV, low:high, 0:lon_cells] = u_ref[...]
    wind[LEV : 2 * LEV, low:high, 0:lon_cells] = v_ref[...]
    pl.semaphore_wait(barrier, devices - 1)

    def lat_pair(buffer, send, recv):
        down = pltpu.make_async_remote_copy(
            src_ref=buffer.at[:, low : low + EDGE, 0:lon_cells],
            dst_ref=buffer.at[:, high : high + EDGE, 0:lon_cells],
            send_sem=send.at[0], recv_sem=recv.at[0], device_id=lat_down, device_id_type=MESH,
        )
        up = pltpu.make_async_remote_copy(
            src_ref=buffer.at[:, high - EDGE : high, 0:lon_cells],
            dst_ref=buffer.at[:, 0:low, 0:lon_cells],
            send_sem=send.at[1], recv_sem=recv.at[1], device_id=lat_up, device_id_type=MESH,
        )
        return down, up

    def lon_pair(send_buf, got_buf, send, recv):
        down = pltpu.make_async_remote_copy(
            src_ref=send_buf.at[0], dst_ref=got_buf.at[0],
            send_sem=send.at[0], recv_sem=recv.at[0], device_id=lon_down, device_id_type=MESH,
        )
        up = pltpu.make_async_remote_copy(
            src_ref=send_buf.at[1], dst_ref=got_buf.at[1],
            send_sem=send.at[1], recv_sem=recv.at[1], device_id=lon_up, device_id_type=MESH,
        )
        return down, up

    lane = lax.broadcasted_iota(jnp.int32, (tall, lon_cells), 1)

    def pack(source, count, target):
        first = jnp.zeros((tall, lon_cells), jnp.float32)
        last = first
        for c in range(count):
            body = source[c, :, 0:lon_cells]
            here = (lane >= EDGE * c) & (lane < EDGE * (c + 1))
            a = body if c == 0 else pltpu.roll(body, EDGE * c, 1)
            shift = (EDGE * (c + 1)) % lon_cells
            b = body if shift == 0 else pltpu.roll(body, shift, 1)
            first = jnp.where(here, a, first)
            last = jnp.where(here, b, last)
        target[0] = first
        target[1] = last

    def unpack(got, count, target):
        after, before = got[0], got[1]
        for c in range(count):
            back = (lon_cells - EDGE * c) % lon_cells
            a = after if back == 0 else pltpu.roll(after, back, 1)
            shift = (lon_cells - EDGE - EDGE * c) % lon_cells
            b = before if shift == 0 else pltpu.roll(before, shift, 1)
            target[c, :, lon_cells : 2 * lon_cells] = jnp.where(lane < EDGE, a, b)

    def field_lat(s):
        return lat_pair(field.at[s], flat_send.at[s], flat_recv.at[s])

    def field_lon(s):
        return lon_pair(lon_send.at[s], lon_got.at[s], flon_send.at[s], flon_recv.at[s])

    def send_slot(s):
        @pl.loop(1, devices)
        def _(k):
            to = (me + k) % devices
            pltpu.make_async_remote_copy(
                src_ref=innov_ref.at[s, to], dst_ref=got_innov.at[s, k],
                send_sem=innov_send.at[s], recv_sem=innov_recv.at[s],
                device_id=(to // n_lat, to % n_lat), device_id_type=MESH,
            ).start()

    def slot_total(s):
        return pltpu.make_async_remote_copy(
            src_ref=got_innov.at[s, 1:devices], dst_ref=got_innov.at[s, 1:devices],
            send_sem=innov_send.at[s], recv_sem=innov_recv.at[s], device_id=lat_up, device_id_type=MESH,
        )

    def send_meta(m):
        @pl.loop(1, devices)
        def _(k):
            to = (me + k) % devices
            pltpu.make_async_remote_copy(
                src_ref=meta_ref.at[m, to], dst_ref=got_meta.at[m, k],
                send_sem=meta_send.at[m], recv_sem=meta_recv.at[m],
                device_id=(to // n_lat, to % n_lat), device_id_type=MESH,
            ).start()

    def meta_total(m):
        return pltpu.make_async_remote_copy(
            src_ref=got_meta.at[m, 1:devices], dst_ref=got_meta.at[m, 1:devices],
            send_sem=meta_send.at[m], recv_sem=meta_recv.at[m], device_id=lat_up, device_id_type=MESH,
        )

    wind_lat = lat_pair(wind, wlat_send, wlat_recv)
    wind_lon = lon_pair(wind_send, wind_got, wlon_send, wlon_recv)
    for copy in wind_lat:
        copy.start()
    send_meta(0)
    for n in range(AHEAD):
        send_slot(slots - 1 - n)
    own_a.wait()
    own_b.wait()
    for copy in wind_lat:
        copy.wait()
    pack(wind, 2 * LEV, wind_send)
    for copy in wind_lon:
        copy.start()

    row_id = lax.broadcasted_iota(jnp.int32, (lat_cells, span), 0).astype(jnp.float32)
    col_id = lax.broadcasted_iota(jnp.int32, (lon_cells, span), 0).astype(jnp.float32)
    contract = (((1,), (1,)), ((), ()))
    row_at = lax.broadcasted_iota(jnp.int32, (tall, 2 * lon_cells), 0)
    first_row = jnp.where(my_lat == 0, low, 0)
    last_row = jnp.where(my_lat == n_lat - 1, high, tall)
    inside = (row_at >= first_row) & (row_at < last_row)

    def stepped(older, c):
        total = mix_ref[0, c] * field[older, 0]
        for d in range(1, CH):
            total = total + mix_ref[d, c] * field[older, d]
        total = jnp.where(inside, total, 0.0)
        level = c % LEV
        eastward = (0.5 * wind[level]) * total
        northward = (0.5 * wind[LEV + level]) * total
        near = KAPPA * total
        return (
            (1.0 - 4.0 * KAPPA) * total
            + pltpu.roll(near + eastward, 2 * lon_cells - 1, 1)
            + pltpu.roll(near - eastward, 1, 1)
            + pltpu.roll(near + northward, tall - 1, 0)
            + pltpu.roll(near - northward, 1, 0)
        )

    def take_meta(m):
        meta_total(m).wait_recv()

        @pl.loop(0, devices // GROUP)
        def _(g):
            for i in range(GROUP):
                numbers = got_meta[m, g * GROUP + i].astype(jnp.float32)
                for j in range(4):
                    s = slots - 1 - (4 * m + j)
                    if s >= 0:
                        rows_buf[s, g, 0:4, i * width : (i + 1) * width] = numbers[4 * j : 4 * j + 4]

    def gather_slot(s):
        acc[...] = jnp.zeros(acc.shape, jnp.float32)

        @pl.loop(0, devices // GROUP)
        def _(g):
            values = jnp.concatenate(
                [got_innov[s, g * GROUP + i] for i in range(GROUP)], axis=1
            ).astype(jnp.float32)
            frac_y, frac_x = rows_buf[s, g, 0:1], rows_buf[s, g, 1:2]
            row, col = rows_buf[s, g, 2:3], rows_buf[s, g, 3:4]
            at_row = jnp.where(row_id == row, 1.0, 0.0).astype(jnp.bfloat16)
            at_next = jnp.where(row_id == row + 1.0, 1.0, 0.0).astype(jnp.bfloat16)
            hit = col_id == col
            cols = jnp.concatenate(
                [jnp.where(hit, 1.0, 0.0).astype(jnp.bfloat16), jnp.where(hit, frac_x, 0.0).astype(jnp.bfloat16)], axis=0
            )
            lower = values * (1.0 - frac_y)
            upper = values * frac_y
            lower_hi = lower.astype(jnp.bfloat16).astype(jnp.float32)
            upper_hi = upper.astype(jnp.bfloat16).astype(jnp.float32)
            lower_lo = lower - lower_hi
            upper_lo = upper - upper_hi

            def spread(low_part, up_part):
                pieces = []
                for c in range(CH):
                    a = jnp.broadcast_to(low_part[c : c + 1], (16, span)).astype(jnp.bfloat16)
                    b = jnp.broadcast_to(up_part[c : c + 1], (16, span)).astype(jnp.bfloat16)
                    for r in range(0, lat_cells, 16):
                        pieces.append(a * at_row[r : r + 16] + b * at_next[r : r + 16])
                return jnp.concatenate(pieces, axis=0)

            total = lax.dot_general(
                spread(lower_hi, upper_hi), cols, contract, preferred_element_type=jnp.float32
            )
            total = total + lax.dot_general(
                spread(lower_lo, upper_lo), cols, contract, preferred_element_type=jnp.float32
            )
            acc[...] += total

        plain = acc[:, 0:lon_cells]
        part = acc[:, lon_cells : 2 * lon_cells]
        whole = plain - part + pltpu.roll(part, 1, 1)
        field[s, :, low:high, 0:lon_cells] = whole.reshape(CH, lat_cells, lon_cells)

    @pl.loop(0, slots)
    def _(n):
        s = slots - 1 - n

        @pl.when(n >= 1)
        def _():
            for copy in field_lat(s + 1):
                copy.wait()
            pack(field.at[s + 1], CH, lon_send.at[s + 1])
            for copy in field_lon(s + 1):
                copy.start()

        slot_total(s).wait_recv()

        @pl.when(n + AHEAD < slots)
        def _():
            send_slot(s - AHEAD)

        for m in range(1, metas):

            @pl.when(n + AHEAD == 4 * m)
            def _():
                send_meta(m)

        for m in range(metas):

            @pl.when(n == 4 * m)
            def _():
                take_meta(m)

        gather_slot(s)

        @pl.when(n < slots - 1)
        def _():
            for copy in field_lat(s):
                copy.start()

        @pl.when(n == 1)
        def _():
            for copy in wind_lon:
                copy.wait()
            unpack(wind_got, 2 * LEV, wind)

        @pl.when(n >= 1)
        def _():
            for copy in field_lon(s + 1):
                copy.wait_recv()
            unpack(lon_got.at[s + 1], CH, field.at[s + 1])

        @pl.when(n >= 2)
        def _():
            @pl.loop(0, CH)
            def _(c):
                field[s + 1, c] += stepped(s + 2, c)

    @pl.loop(0, CH)
    def _(c):
        out_ref[c] = stepped(1, c)[low:high, 0:lon_cells] + field[0, c, low:high, 0:lon_cells]

    @pl.loop(0, slots)
    def _(s):
        slot_total(s).wait_send()

        @pl.when(s > 0)
        def _():
            for copy in field_lon(s):
                copy.wait_send()

    for m in range(metas):
        meta_total(m).wait_send()


def shards(n_lon, n_lat, innovations, fractions, cell_index, counts, blocks, u_wind, v_wind, channel_mix):
    slots, devices, channels, width = innovations.shape
    lat_cells, lon_cells = u_wind.shape[1:]
    across = lon_cells // TILE
    tiles = counts.shape[2]
    per_tile = width // tiles
    within = lax.broadcasted_iota(jnp.int32, (1, 1, tiles, per_tile), 3)
    live = within < counts[..., None]
    cell = cell_index.reshape(slots, devices, tiles, per_tile)
    block = blocks[..., None]
    row = jnp.where(live, (block // across) * TILE + cell // TILE, -100)
    col = (block % across) * TILE + cell % TILE
    places = jnp.stack([row, col], axis=2).reshape(slots, devices, 2, width).astype(jnp.bfloat16)
    meta = jnp.concatenate([fractions, places], axis=2)
    metas = -(-slots // 4)
    meta = jnp.pad(meta[::-1], ((0, 4 * metas - slots), (0, 0), (0, 0), (0, 0)))
    meta = meta.reshape(metas, 4, devices, 4, width)
    meta = jnp.transpose(meta, (0, 2, 1, 3, 4)).reshape(metas, devices, 16, width)

    tall, wide = lat_cells + 2 * EDGE, 2 * lon_cells
    f32, bf16, dma = jnp.float32, jnp.bfloat16, pltpu.SemaphoreType.DMA
    vmem = pl.BlockSpec(memory_space=pltpu.VMEM)
    out = pl.pallas_call(
        functools.partial(kernel, n_lon, n_lat, slots, lat_cells, lon_cells),
        out_shape=jax.ShapeDtypeStruct((CH, lat_cells, lon_cells), f32),
        in_specs=[
            pl.BlockSpec(memory_space=pltpu.SMEM),
            pl.BlockSpec(memory_space=pl.ANY),
            pl.BlockSpec(memory_space=pl.ANY),
            vmem,
            vmem,
        ],
        out_specs=vmem,
        scratch_shapes=[
            pltpu.VMEM((slots, devices, channels, width), bf16),
            pltpu.VMEM((metas, devices, 16, width), bf16),
            pltpu.VMEM((slots, devices // GROUP, 8, GROUP * width), f32),
            pltpu.VMEM((CH * lat_cells, wide), f32),
            pltpu.VMEM((slots, CH, tall, wide), f32),
            pltpu.VMEM((2 * LEV, tall, wide), f32),
            pltpu.VMEM((2, tall, lon_cells), f32),
            pltpu.VMEM((2, tall, lon_cells), f32),
            pltpu.VMEM((slots, 2, tall, lon_cells), f32),
            pltpu.VMEM((slots, 2, tall, lon_cells), f32),
            dma((2,)),
            dma((slots,)),
            dma((slots,)),
            dma((metas,)),
            dma((metas,)),
            dma((2,)),
            dma((2,)),
            dma((2,)),
            dma((2,)),
            dma((slots, 2)),
            dma((slots, 2)),
            dma((slots, 2)),
            dma((slots, 2)),
        ],
        compiler_params=pltpu.CompilerParams(
            collective_id=0, has_side_effects=True, vmem_limit_bytes=48 * 1024 * 1024
        ),
    )(channel_mix, innovations, meta, u_wind, v_wind)
    return out.reshape(VARS, LEV, lat_cells, lon_cells)


def solution(mesh):
    in_specs = (
        P(None, ("lon", "lat"), None, None),
        P(None, ("lon", "lat"), None, None),
        P(None, ("lon", "lat"), None),
        P(None, ("lon", "lat"), None),
        P(None, ("lon", "lat"), None),
        P(None, "lat", "lon"),
        P(None, "lat", "lon"),
        P(),
    )
    out_specs = P(None, None, "lat", "lon")
    body = functools.partial(shards, mesh.shape["lon"], mesh.shape["lat"])
    return jax.shard_map(body, mesh=mesh, in_specs=in_specs, out_specs=out_specs, check_vma=False)
```

```python
import functools

import jax
import jax.numpy as jnp
from jax import lax
from jax.experimental import pallas as pl
from jax.experimental.pallas import tpu as pltpu
from jax.sharding import PartitionSpec as P

VARS = 4
LEV = 4
CH = 16
TILE = 16
KAPPA = 0.125
EDGE = 8
GROUP = 4
AHEAD = 2
MESH = pl.DeviceIdType.MESH


def kernel(
    n_lon, n_lat, slots, lat_cells, lon_cells,
    mix_ref, innov_ref, meta_ref, u_ref, v_ref, out_ref,
    got_innov, got_meta, rows_buf, acc, field, wind, wind_send, wind_got, lon_send, lon_got,
    own_sem, innov_send, innov_recv, meta_send, meta_recv,
    wlat_send, wlat_recv, wlon_send, wlon_recv, flat_send, flat_recv, flon_send, flon_recv,
):
    devices = n_lon * n_lat
    my_lon, my_lat = lax.axis_index("lon"), lax.axis_index("lat")
    me = my_lon * n_lat + my_lat
    width = got_innov.shape[-1]
    span = GROUP * width
    tall = lat_cells + 2 * EDGE
    low, high = EDGE, EDGE + lat_cells
    metas = got_meta.shape[0]

    lat_up = (my_lon, (my_lat + 1) % n_lat)
    lat_down = (my_lon, (my_lat + n_lat - 1) % n_lat)
    lon_up = ((my_lon + 1) % n_lon, my_lat)
    lon_down = ((my_lon + n_lon - 1) % n_lon, my_lat)

    barrier = pltpu.get_barrier_semaphore()

    @pl.loop(1, devices)
    def _(k):
        to = (me + k) % devices
        pl.semaphore_signal(barrier, inc=1, device_id=(to // n_lat, to % n_lat), device_id_type=MESH)

    own_a = pltpu.make_async_copy(innov_ref.at[:, me], got_innov.at[:, 0], own_sem.at[0])
    own_b = pltpu.make_async_copy(meta_ref.at[:, me], got_meta.at[:, 0], own_sem.at[1])
    own_a.start()
    own_b.start()
    wind[0:LEV, low:high, 0:lon_cells] = u_ref[...]
    wind[LEV : 2 * LEV, low:high, 0:lon_cells] = v_ref[...]
    pl.semaphore_wait(barrier, devices - 1)

    def lat_pair(buffer, send, recv):
        down = pltpu.make_async_remote_copy(
            src_ref=buffer.at[:, low : low + EDGE, 0:lon_cells],
            dst_ref=buffer.at[:, high : high + EDGE, 0:lon_cells],
            send_sem=send.at[0], recv_sem=recv.at[0], device_id=lat_down, device_id_type=MESH,
        )
        up = pltpu.make_async_remote_copy(
            src_ref=buffer.at[:, high - EDGE : high, 0:lon_cells],
            dst_ref=buffer.at[:, 0:low, 0:lon_cells],
            send_sem=send.at[1], recv_sem=recv.at[1], device_id=lat_up, device_id_type=MESH,
        )
        return down, up

    def lon_pair(send_buf, got_buf, send, recv):
        down = pltpu.make_async_remote_copy(
            src_ref=send_buf.at[0], dst_ref=got_buf.at[0],
            send_sem=send.at[0], recv_sem=recv.at[0], device_id=lon_down, device_id_type=MESH,
        )
        up = pltpu.make_async_remote_copy(
            src_ref=send_buf.at[1], dst_ref=got_buf.at[1],
            send_sem=send.at[1], recv_sem=recv.at[1], device_id=lon_up, device_id_type=MESH,
        )
        return down, up

    lane = lax.broadcasted_iota(jnp.int32, (tall, lon_cells), 1)

    def pack(source, count, target):
        first = jnp.zeros((tall, lon_cells), jnp.float32)
        last = first
        for c in range(count):
            body = source[c, :, 0:lon_cells]
            here = (lane >= EDGE * c) & (lane < EDGE * (c + 1))
            a = body if c == 0 else pltpu.roll(body, EDGE * c, 1)
            shift = (EDGE * (c + 1)) % lon_cells
            b = body if shift == 0 else pltpu.roll(body, shift, 1)
            first = jnp.where(here, a, first)
            last = jnp.where(here, b, last)
        target[0] = first
        target[1] = last

    def unpack(got, count, target):
        after, before = got[0], got[1]
        for c in range(count):
            back = (lon_cells - EDGE * c) % lon_cells
            a = after if back == 0 else pltpu.roll(after, back, 1)
            shift = (lon_cells - EDGE - EDGE * c) % lon_cells
            b = before if shift == 0 else pltpu.roll(before, shift, 1)
            target[c, :, lon_cells : 2 * lon_cells] = jnp.where(lane < EDGE, a, b)

    def field_lat(s):
        return lat_pair(field.at[s], flat_send.at[s], flat_recv.at[s])

    def field_lon(s):
        return lon_pair(lon_send.at[s], lon_got.at[s], flon_send.at[s], flon_recv.at[s])

    def send_slot(s):
        @pl.loop(1, devices)
        def _(k):
            to = (me + k) % devices
            pltpu.make_async_remote_copy(
                src_ref=innov_ref.at[s, to], dst_ref=got_innov.at[s, k],
                send_sem=innov_send.at[s], recv_sem=innov_recv.at[s],
                device_id=(to // n_lat, to % n_lat), device_id_type=MESH,
            ).start()

    def slot_total(s):
        return pltpu.make_async_remote_copy(
            src_ref=got_innov.at[s, 1:devices], dst_ref=got_innov.at[s, 1:devices],
            send_sem=innov_send.at[s], recv_sem=innov_recv.at[s], device_id=lat_up, device_id_type=MESH,
        )

    def send_meta(m):
        @pl.loop(1, devices)
        def _(k):
            to = (me + k) % devices
            pltpu.make_async_remote_copy(
                src_ref=meta_ref.at[m, to], dst_ref=got_meta.at[m, k],
                send_sem=meta_send.at[m], recv_sem=meta_recv.at[m],
                device_id=(to // n_lat, to % n_lat), device_id_type=MESH,
            ).start()

    def meta_total(m):
        return pltpu.make_async_remote_copy(
            src_ref=got_meta.at[m, 1:devices], dst_ref=got_meta.at[m, 1:devices],
            send_sem=meta_send.at[m], recv_sem=meta_recv.at[m], device_id=lat_up, device_id_type=MESH,
        )

    wind_lat = lat_pair(wind, wlat_send, wlat_recv)
    wind_lon = lon_pair(wind_send, wind_got, wlon_send, wlon_recv)
    for copy in wind_lat:
        copy.start()
    send_meta(0)
    for n in range(AHEAD):
        send_slot(slots - 1 - n)
    own_a.wait()
    own_b.wait()
    for copy in wind_lat:
        copy.wait()
    pack(wind, 2 * LEV, wind_send)
    for copy in wind_lon:
        copy.start()

    across = lon_cells // TILE
    tile_id = lax.broadcasted_iota(jnp.int32, (TILE, span), 0).astype(jnp.float32)
    lane_group = lax.broadcasted_iota(jnp.int32, (CH, lon_cells), 1) // TILE
    contract = (((1,), (1,)), ((), ()))
    row_at = lax.broadcasted_iota(jnp.int32, (tall, 2 * lon_cells), 0)
    first_row = jnp.where(my_lat == 0, low, 0)
    last_row = jnp.where(my_lat == n_lat - 1, high, tall)
    inside = (row_at >= first_row) & (row_at < last_row)

    def stepped(older, c):
        total = mix_ref[0, c] * field[older, 0]
        for d in range(1, CH):
            total = total + mix_ref[d, c] * field[older, d]
        total = jnp.where(inside, total, 0.0)
        level = c % LEV
        eastward = (0.5 * wind[level]) * total
        northward = (0.5 * wind[LEV + level]) * total
        near = KAPPA * total
        return (
            (1.0 - 4.0 * KAPPA) * total
            + pltpu.roll(near + eastward, 2 * lon_cells - 1, 1)
            + pltpu.roll(near - eastward, 1, 1)
            + pltpu.roll(near + northward, tall - 1, 0)
            + pltpu.roll(near - northward, 1, 0)
        )

    def take_meta(m):
        meta_total(m).wait_recv()

        @pl.loop(0, devices // GROUP)
        def _(g):
            for i in range(GROUP):
                numbers = got_meta[m, g * GROUP + i].astype(jnp.float32)
                for j in range(4):
                    s = slots - 1 - (4 * m + j)
                    if s >= 0:
                        rows_buf[s, g, 0:4, i * width : (i + 1) * width] = numbers[4 * j : 4 * j + 4]

    def gather_slot(s):
        acc[...] = jnp.zeros(acc.shape, jnp.float32)

        @pl.loop(0, devices // GROUP)
        def _(g):
            values = jnp.concatenate(
                [got_innov[s, g * GROUP + i] for i in range(GROUP)], axis=1
            )
            frac_y, frac_x = rows_buf[s, g, 0:1], rows_buf[s, g, 1:2]
            cell, block = rows_buf[s, g, 2:3], rows_buf[s, g, 3:4]
            row = jnp.floor(cell * (1.0 / TILE))
            col = cell - TILE * row
            in_rows = jnp.where(tile_id == row, 1.0 - frac_y, jnp.where(tile_id == row + 1.0, frac_y, 0.0))
            in_cols = jnp.where(tile_id == col, 1.0 - frac_x, jnp.where(tile_id == col + 1.0, frac_x, 0.0))
            heads, tails = [], []
            for r in range(TILE):
                weight = in_rows[r : r + 1] * in_cols
                head = weight.astype(jnp.bfloat16)
                heads.append(head)
                tails.append((weight - head.astype(jnp.float32)).astype(jnp.bfloat16))
            weights = jnp.concatenate(heads + tails, axis=0)
            placed = []
            for b in range(lat_cells // TILE * across):
                here = jnp.broadcast_to(jnp.where(block == float(b), 1.0, 0.0), (CH, span)).astype(jnp.bfloat16)
                placed.append(values * here)
            placed = jnp.concatenate(placed, axis=0)
            both = lax.dot_general(weights, placed, contract, preferred_element_type=jnp.float32)
            acc[...] += both[: TILE * TILE] + both[TILE * TILE :]

        tiles = jnp.transpose(acc[...])
        strips = []
        for down in range(lat_cells // TILE):
            for half in range(TILE // across):
                x = []
                for i in range(across):
                    b = down * across + i
                    x.append(tiles[b * CH : (b + 1) * CH, half * lon_cells : (half + 1) * lon_cells])
                apart = 1
                while apart < across:
                    moved = list(x)
                    for i in range(across):
                        if i & apart == 0:
                            j = i + apart
                            moved[i] = jnp.where(lane_group & apart == 0, x[i], pltpu.roll(x[j], TILE * apart, 1))
                            moved[j] = jnp.where(
                                lane_group & apart == 0, pltpu.roll(x[i], lon_cells - TILE * apart, 1), x[j]
                            )
                    x = moved
                    apart *= 2
                strips += x
        whole = jnp.stack(strips, axis=0)
        field[s, :, low:high, 0:lon_cells] = jnp.swapaxes(whole, 0, 1)

    @pl.loop(0, slots)
    def _(n):
        s = slots - 1 - n

        @pl.when(n >= 1)
        def _():
            for copy in field_lat(s + 1):
                copy.wait()
            pack(field.at[s + 1], CH, lon_send.at[s + 1])
            for copy in field_lon(s + 1):
                copy.start()

        slot_total(s).wait_recv()

        @pl.when(n + AHEAD < slots)
        def _():
            send_slot(s - AHEAD)

        for m in range(1, metas):

            @pl.when(n + AHEAD == 4 * m)
            def _():
                send_meta(m)

        for m in range(metas):

            @pl.when(n == 4 * m)
            def _():
                take_meta(m)

        gather_slot(s)

        @pl.when(n < slots - 1)
        def _():
            for copy in field_lat(s):
                copy.start()

        @pl.when(n == 1)
        def _():
            for copy in wind_lon:
                copy.wait()
            unpack(wind_got, 2 * LEV, wind)

        @pl.when(n >= 1)
        def _():
            for copy in field_lon(s + 1):
                copy.wait_recv()
            unpack(lon_got.at[s + 1], CH, field.at[s + 1])

        @pl.when(n >= 2)
        def _():
            @pl.loop(0, CH)
            def _(c):
                field[s + 1, c] += stepped(s + 2, c)

    @pl.loop(0, CH)
    def _(c):
        out_ref[c] = stepped(1, c)[low:high, 0:lon_cells] + field[0, c, low:high, 0:lon_cells]

    @pl.loop(0, slots)
    def _(s):
        slot_total(s).wait_send()

        @pl.when(s > 0)
        def _():
            for copy in field_lon(s):
                copy.wait_send()

    for m in range(metas):
        meta_total(m).wait_send()


def shards(n_lon, n_lat, innovations, fractions, cell_index, counts, blocks, u_wind, v_wind, channel_mix):
    slots, devices, channels, width = innovations.shape
    lat_cells, lon_cells = u_wind.shape[1:]
    tiles = counts.shape[2]
    per_tile = width // tiles
    within = lax.broadcasted_iota(jnp.int32, (1, 1, tiles, per_tile), 3)
    live = within < counts[..., None]
    block = jnp.where(live, blocks[..., None], -1).reshape(slots, devices, width)
    places = jnp.stack([cell_index, block], axis=2).astype(jnp.bfloat16)
    meta = jnp.concatenate([fractions, places], axis=2)
    metas = -(-slots // 4)
    meta = jnp.pad(meta[::-1], ((0, 4 * metas - slots), (0, 0), (0, 0), (0, 0)))
    meta = meta.reshape(metas, 4, devices, 4, width)
    meta = jnp.transpose(meta, (0, 2, 1, 3, 4)).reshape(metas, devices, 16, width)

    tall, wide = lat_cells + 2 * EDGE, 2 * lon_cells
    f32, bf16, dma = jnp.float32, jnp.bfloat16, pltpu.SemaphoreType.DMA
    vmem = pl.BlockSpec(memory_space=pltpu.VMEM)
    out = pl.pallas_call(
        functools.partial(kernel, n_lon, n_lat, slots, lat_cells, lon_cells),
        out_shape=jax.ShapeDtypeStruct((CH, lat_cells, lon_cells), f32),
        in_specs=[
            pl.BlockSpec(memory_space=pltpu.SMEM),
            pl.BlockSpec(memory_space=pl.ANY),
            pl.BlockSpec(memory_space=pl.ANY),
            vmem,
            vmem,
        ],
        out_specs=vmem,
        scratch_shapes=[
            pltpu.VMEM((slots, devices, channels, width), bf16),
            pltpu.VMEM((metas, devices, 16, width), bf16),
            pltpu.VMEM((slots, devices // GROUP, 8, GROUP * width), f32),
            pltpu.VMEM((TILE * TILE, CH * lat_cells * lon_cells // TILE**2), f32),
            pltpu.VMEM((slots, CH, tall, wide), f32),
            pltpu.VMEM((2 * LEV, tall, wide), f32),
            pltpu.VMEM((2, tall, lon_cells), f32),
            pltpu.VMEM((2, tall, lon_cells), f32),
            pltpu.VMEM((slots, 2, tall, lon_cells), f32),
            pltpu.VMEM((slots, 2, tall, lon_cells), f32),
            dma((2,)),
            dma((slots,)),
            dma((slots,)),
            dma((metas,)),
            dma((metas,)),
            dma((2,)),
            dma((2,)),
            dma((2,)),
            dma((2,)),
            dma((slots, 2)),
            dma((slots, 2)),
            dma((slots, 2)),
            dma((slots, 2)),
        ],
        compiler_params=pltpu.CompilerParams(
            collective_id=0, has_side_effects=True, vmem_limit_bytes=48 * 1024 * 1024
        ),
    )(channel_mix, innovations, meta, u_wind, v_wind)
    return out.reshape(VARS, LEV, lat_cells, lon_cells)


def solution(mesh):
    in_specs = (
        P(None, ("lon", "lat"), None, None),
        P(None, ("lon", "lat"), None, None),
        P(None, ("lon", "lat"), None),
        P(None, ("lon", "lat"), None),
        P(None, ("lon", "lat"), None),
        P(None, "lat", "lon"),
        P(None, "lat", "lon"),
        P(),
    )
    out_specs = P(None, None, "lat", "lon")
    body = functools.partial(shards, mesh.shape["lon"], mesh.shape["lat"])
    return jax.shard_map(body, mesh=mesh, in_specs=in_specs, out_specs=out_specs, check_vma=False)
```

```python
import functools

import jax
import jax.numpy as jnp
from jax import lax
from jax.experimental import pallas as pl
from jax.experimental.pallas import tpu as pltpu
from jax.sharding import PartitionSpec as P

VARS = 4
LEV = 4
CH = 16
TILE = 16
KAPPA = 0.125
EDGE = 8
GROUP = 4
WAVES = 3
MESH = pl.DeviceIdType.MESH


def kernel(
    n_lon, n_lat, slots, lat_cells, lon_cells,
    mix_ref, innov_ref, meta_ref, u_ref, v_ref, out_ref,
    got_innov, got_meta, rows_buf, acc, field, wind, wind_send, wind_got, lon_send, lon_got,
    own_sem, innov_send, innov_recv, meta_send, meta_recv,
    wlat_send, wlat_recv, wlon_send, wlon_recv, flat_send, flat_recv, flon_send, flon_recv,
):
    devices = n_lon * n_lat
    my_lon, my_lat = lax.axis_index("lon"), lax.axis_index("lat")
    me = my_lon * n_lat + my_lat
    width = got_innov.shape[-1]
    span = GROUP * width
    tall = lat_cells + 2 * EDGE
    low, high = EDGE, EDGE + lat_cells
    cuts = [slots - (slots * w + WAVES - 1) // WAVES for w in range(WAVES + 1)]
    waves = [(end, first) for first, end in zip(cuts, cuts[1:])]

    lat_up = (my_lon, (my_lat + 1) % n_lat)
    lat_down = (my_lon, (my_lat + n_lat - 1) % n_lat)
    lon_up = ((my_lon + 1) % n_lon, my_lat)
    lon_down = ((my_lon + n_lon - 1) % n_lon, my_lat)

    barrier = pltpu.get_barrier_semaphore()

    @pl.loop(1, devices)
    def _(k):
        to = (me + k) % devices
        pl.semaphore_signal(barrier, inc=1, device_id=(to // n_lat, to % n_lat), device_id_type=MESH)

    own_a = pltpu.make_async_copy(innov_ref.at[:, me], got_innov.at[:, 0], own_sem.at[0])
    own_b = pltpu.make_async_copy(meta_ref.at[me], got_meta.at[0], own_sem.at[1])
    own_a.start()
    own_b.start()
    wind[0:LEV, low:high, 0:lon_cells] = u_ref[...]
    wind[LEV : 2 * LEV, low:high, 0:lon_cells] = v_ref[...]
    pl.semaphore_wait(barrier, devices - 1)

    def lat_pair(buffer, send, recv):
        down = pltpu.make_async_remote_copy(
            src_ref=buffer.at[:, low : low + EDGE, 0:lon_cells],
            dst_ref=buffer.at[:, high : high + EDGE, 0:lon_cells],
            send_sem=send.at[0], recv_sem=recv.at[0], device_id=lat_down, device_id_type=MESH,
        )
        up = pltpu.make_async_remote_copy(
            src_ref=buffer.at[:, high - EDGE : high, 0:lon_cells],
            dst_ref=buffer.at[:, 0:low, 0:lon_cells],
            send_sem=send.at[1], recv_sem=recv.at[1], device_id=lat_up, device_id_type=MESH,
        )
        return down, up

    def lon_pair(send_buf, got_buf, send, recv):
        down = pltpu.make_async_remote_copy(
            src_ref=send_buf.at[0], dst_ref=got_buf.at[0],
            send_sem=send.at[0], recv_sem=recv.at[0], device_id=lon_down, device_id_type=MESH,
        )
        up = pltpu.make_async_remote_copy(
            src_ref=send_buf.at[1], dst_ref=got_buf.at[1],
            send_sem=send.at[1], recv_sem=recv.at[1], device_id=lon_up, device_id_type=MESH,
        )
        return down, up

    lane = lax.broadcasted_iota(jnp.int32, (tall, lon_cells), 1)

    def pack(source, count, target):
        first = jnp.zeros((tall, lon_cells), jnp.float32)
        last = first
        for c in range(count):
            body = source[c, :, 0:lon_cells]
            here = (lane >= EDGE * c) & (lane < EDGE * (c + 1))
            a = body if c == 0 else pltpu.roll(body, EDGE * c, 1)
            shift = (EDGE * (c + 1)) % lon_cells
            b = body if shift == 0 else pltpu.roll(body, shift, 1)
            first = jnp.where(here, a, first)
            last = jnp.where(here, b, last)
        target[0] = first
        target[1] = last

    def unpack(got, count, target):
        after, before = got[0], got[1]
        for c in range(count):
            back = (lon_cells - EDGE * c) % lon_cells
            a = after if back == 0 else pltpu.roll(after, back, 1)
            shift = (lon_cells - EDGE - EDGE * c) % lon_cells
            b = before if shift == 0 else pltpu.roll(before, shift, 1)
            target[c, :, lon_cells : 2 * lon_cells] = jnp.where(lane < EDGE, a, b)

    def field_lat(s):
        return lat_pair(field.at[s], flat_send.at[s], flat_recv.at[s])

    def field_lon(s):
        return lon_pair(lon_send.at[s], lon_got.at[s], flon_send.at[s], flon_recv.at[s])

    def wave(w, k, to):
        first, end = waves[w]
        return pltpu.make_async_remote_copy(
            src_ref=innov_ref.at[first:end, to], dst_ref=got_innov.at[first:end, k],
            send_sem=innov_send.at[w], recv_sem=innov_recv.at[w],
            device_id=(to // n_lat, to % n_lat), device_id_type=MESH,
        )

    def wave_total(w):
        first, end = waves[w]
        whole = got_innov.at[first:end, 1:devices]
        return pltpu.make_async_remote_copy(
            src_ref=whole, dst_ref=whole,
            send_sem=innov_send.at[w], recv_sem=innov_recv.at[w], device_id=lat_up, device_id_type=MESH,
        )

    def meta_copy(k, to):
        return pltpu.make_async_remote_copy(
            src_ref=meta_ref.at[to], dst_ref=got_meta.at[k],
            send_sem=meta_send.at[0], recv_sem=meta_recv.at[0],
            device_id=(to // n_lat, to % n_lat), device_id_type=MESH,
        )

    def meta_total():
        whole = got_meta.at[1:devices]
        return pltpu.make_async_remote_copy(
            src_ref=whole, dst_ref=whole,
            send_sem=meta_send.at[0], recv_sem=meta_recv.at[0], device_id=lat_up, device_id_type=MESH,
        )

    wind_lat = lat_pair(wind, wlat_send, wlat_recv)
    wind_lon = lon_pair(wind_send, wind_got, wlon_send, wlon_recv)
    for copy in wind_lat:
        copy.start()

    @pl.loop(1, devices)
    def _(k):
        to = (me + k) % devices
        meta_copy(k, to).start()
        wave(0, k, to).start()

    for w in range(1, len(waves)):

        @pl.loop(1, devices)
        def _(k):
            wave(w, k, (me + k) % devices).start()

    own_a.wait()
    own_b.wait()
    for copy in wind_lat:
        copy.wait()
    pack(wind, 2 * LEV, wind_send)
    for copy in wind_lon:
        copy.start()

    across = lon_cells // TILE
    tile_id = lax.broadcasted_iota(jnp.int32, (TILE, span), 0).astype(jnp.float32)
    lane_group = lax.broadcasted_iota(jnp.int32, (CH, lon_cells), 1) // TILE
    contract = (((1,), (1,)), ((), ()))
    row_at = lax.broadcasted_iota(jnp.int32, (tall, 2 * lon_cells), 0)
    first_row = jnp.where(my_lat == 0, low, 0)
    last_row = jnp.where(my_lat == n_lat - 1, high, tall)
    inside = (row_at >= first_row) & (row_at < last_row)

    def stepped(older, c):
        total = mix_ref[0, c] * field[older, 0]
        for d in range(1, CH):
            total = total + mix_ref[d, c] * field[older, d]
        total = jnp.where(inside, total, 0.0)
        level = c % LEV
        eastward = (0.5 * wind[level]) * total
        northward = (0.5 * wind[LEV + level]) * total
        near = KAPPA * total
        return (
            (1.0 - 4.0 * KAPPA) * total
            + pltpu.roll(near + eastward, 2 * lon_cells - 1, 1)
            + pltpu.roll(near - eastward, 1, 1)
            + pltpu.roll(near + northward, tall - 1, 0)
            + pltpu.roll(near - northward, 1, 0)
        )

    def take_meta():
        meta_total().wait_recv()

        @pl.loop(0, devices // GROUP)
        def _(g):
            for i in range(GROUP):
                numbers = got_meta[g * GROUP + i].astype(jnp.float32)
                for s in range(slots):
                    rows_buf[s, g, 0:4, i * width : (i + 1) * width] = numbers[4 * s : 4 * s + 4]

    def gather_slot(s):
        acc[...] = jnp.zeros(acc.shape, jnp.float32)

        @pl.loop(0, devices // GROUP)
        def _(g):
            values = jnp.concatenate(
                [got_innov[s, g * GROUP + i] for i in range(GROUP)], axis=1
            )
            frac_y, frac_x = rows_buf[s, g, 0:1], rows_buf[s, g, 1:2]
            cell, block = rows_buf[s, g, 2:3], rows_buf[s, g, 3:4]
            row = jnp.floor(cell * (1.0 / TILE))
            col = cell - TILE * row
            in_rows = jnp.where(tile_id == row, 1.0 - frac_y, jnp.where(tile_id == row + 1.0, frac_y, 0.0))
            in_cols = jnp.where(tile_id == col, 1.0 - frac_x, jnp.where(tile_id == col + 1.0, frac_x, 0.0))
            heads, tails = [], []
            for r in range(TILE):
                weight = in_rows[r : r + 1] * in_cols
                head = weight.astype(jnp.bfloat16)
                heads.append(head)
                tails.append((weight - head.astype(jnp.float32)).astype(jnp.bfloat16))
            weights = jnp.concatenate(heads + tails, axis=0)
            placed = []
            for b in range(lat_cells // TILE * across):
                here = jnp.broadcast_to(jnp.where(block == float(b), 1.0, 0.0), (CH, span)).astype(jnp.bfloat16)
                placed.append(values * here)
            placed = jnp.concatenate(placed, axis=0)
            both = lax.dot_general(weights, placed, contract, preferred_element_type=jnp.float32)
            acc[...] += both[: TILE * TILE] + both[TILE * TILE :]

        tiles = jnp.transpose(acc[...])
        strips = []
        for down in range(lat_cells // TILE):
            for half in range(TILE // across):
                x = []
                for i in range(across):
                    b = down * across + i
                    x.append(tiles[b * CH : (b + 1) * CH, half * lon_cells : (half + 1) * lon_cells])
                apart = 1
                while apart < across:
                    moved = list(x)
                    for i in range(across):
                        if i & apart == 0:
                            j = i + apart
                            moved[i] = jnp.where(lane_group & apart == 0, x[i], pltpu.roll(x[j], TILE * apart, 1))
                            moved[j] = jnp.where(
                                lane_group & apart == 0, pltpu.roll(x[i], lon_cells - TILE * apart, 1), x[j]
                            )
                    x = moved
                    apart *= 2
                strips += x
        whole = jnp.stack(strips, axis=0)
        field[s, :, low:high, 0:lon_cells] = jnp.swapaxes(whole, 0, 1)

    def settle(s):
        for copy in field_lon(s):
            copy.wait_recv()
        unpack(lon_got.at[s], CH, field.at[s])

        @pl.when(s < slots - 1)
        def _():
            @pl.loop(0, CH)
            def _(c):
                field[s, c] += stepped(s + 1, c)

    take_meta()

    @pl.loop(0, slots)
    def _(n):
        s = slots - 1 - n
        for w, (_, end) in enumerate(waves):

            @pl.when(s == end - 1)
            def _():
                wave_total(w).wait_recv()

        gather_slot(s)

        @pl.when(s > 0)
        def _():
            for copy in field_lat(s):
                copy.start()

        @pl.when(n >= 1)
        def _():
            for copy in field_lat(s + 1):
                copy.wait()
            pack(field.at[s + 1], CH, lon_send.at[s + 1])
            for copy in field_lon(s + 1):
                copy.start()

        @pl.when(n == 1)
        def _():
            for copy in wind_lon:
                copy.wait()
            unpack(wind_got, 2 * LEV, wind)

        @pl.when(n >= 2)
        def _():
            settle(s + 2)

    settle(1)

    @pl.loop(0, CH)
    def _(c):
        out_ref[c] = stepped(1, c)[low:high, 0:lon_cells] + field[0, c, low:high, 0:lon_cells]

    @pl.loop(1, slots)
    def _(s):
        for copy in field_lon(s):
            copy.wait_send()

    for w in range(len(waves)):
        wave_total(w).wait_send()
    meta_total().wait_send()


def shards(n_lon, n_lat, innovations, fractions, cell_index, counts, blocks, u_wind, v_wind, channel_mix):
    slots, devices, channels, width = innovations.shape
    lat_cells, lon_cells = u_wind.shape[1:]
    tiles = counts.shape[2]
    per_tile = width // tiles
    within = lax.broadcasted_iota(jnp.int32, (1, 1, tiles, per_tile), 3)
    live = within < counts[..., None]
    block = jnp.where(live, blocks[..., None], -1).reshape(slots, devices, width)
    places = jnp.stack([cell_index, block], axis=2).astype(jnp.bfloat16)
    meta = jnp.concatenate([fractions, places], axis=2)
    meta = jnp.transpose(meta, (1, 0, 2, 3)).reshape(devices, 4 * slots, width)
    meta_rows = -(-4 * slots // 16) * 16
    meta = jnp.pad(meta, ((0, 0), (0, meta_rows - 4 * slots), (0, 0)))

    tall, wide = lat_cells + 2 * EDGE, 2 * lon_cells
    f32, bf16, dma = jnp.float32, jnp.bfloat16, pltpu.SemaphoreType.DMA
    vmem = pl.BlockSpec(memory_space=pltpu.VMEM)
    out = pl.pallas_call(
        functools.partial(kernel, n_lon, n_lat, slots, lat_cells, lon_cells),
        out_shape=jax.ShapeDtypeStruct((CH, lat_cells, lon_cells), f32),
        in_specs=[
            pl.BlockSpec(memory_space=pltpu.SMEM),
            pl.BlockSpec(memory_space=pl.ANY),
            pl.BlockSpec(memory_space=pl.ANY),
            vmem,
            vmem,
        ],
        out_specs=vmem,
        scratch_shapes=[
            pltpu.VMEM((slots, devices, channels, width), bf16),
            pltpu.VMEM((devices, meta_rows, width), bf16),
            pltpu.VMEM((slots, devices // GROUP, 8, GROUP * width), f32),
            pltpu.VMEM((TILE * TILE, CH * lat_cells * lon_cells // TILE**2), f32),
            pltpu.VMEM((slots, CH, tall, wide), f32),
            pltpu.VMEM((2 * LEV, tall, wide), f32),
            pltpu.VMEM((2, tall, lon_cells), f32),
            pltpu.VMEM((2, tall, lon_cells), f32),
            pltpu.VMEM((slots, 2, tall, lon_cells), f32),
            pltpu.VMEM((slots, 2, tall, lon_cells), f32),
            dma((2,)),
            dma((WAVES,)),
            dma((WAVES,)),
            dma((1,)),
            dma((1,)),
            dma((2,)),
            dma((2,)),
            dma((2,)),
            dma((2,)),
            dma((slots, 2)),
            dma((slots, 2)),
            dma((slots, 2)),
            dma((slots, 2)),
        ],
        compiler_params=pltpu.CompilerParams(
            collective_id=0, has_side_effects=True, vmem_limit_bytes=48 * 1024 * 1024
        ),
    )(channel_mix, innovations, meta, u_wind, v_wind)
    return out.reshape(VARS, LEV, lat_cells, lon_cells)


def solution(mesh):
    in_specs = (
        P(None, ("lon", "lat"), None, None),
        P(None, ("lon", "lat"), None, None),
        P(None, ("lon", "lat"), None),
        P(None, ("lon", "lat"), None),
        P(None, ("lon", "lat"), None),
        P(None, "lat", "lon"),
        P(None, "lat", "lon"),
        P(),
    )
    out_specs = P(None, None, "lat", "lon")
    body = functools.partial(shards, mesh.shape["lon"], mesh.shape["lat"])
    return jax.shard_map(body, mesh=mesh, in_specs=in_specs, out_specs=out_specs, check_vma=False)
```

```python
import functools

import jax
import jax.numpy as jnp
from jax import lax
from jax.experimental import pallas as pl
from jax.experimental.pallas import tpu as pltpu
from jax.sharding import PartitionSpec as P

VARS = 4
LEV = 4
CH = 16
TILE = 16
KAPPA = 0.125
EDGE = 8
GROUP = 8
SIDE = 2
WAVES = 3
MESH = pl.DeviceIdType.MESH


def kernel(
    n_lon, n_lat, slots, lat_cells, lon_cells,
    mix_ref, innov_ref, meta_ref, u_ref, v_ref, out_ref,
    got_innov, got_meta, rows_buf, acc, field, wind, wind_send, wind_got, lon_send, lon_got,
    own_sem, innov_send, innov_recv, meta_send, meta_recv,
    wlat_send, wlat_recv, wlon_send, wlon_recv, flat_send, flat_recv, flon_send, flon_recv,
):
    devices = n_lon * n_lat
    my_lon, my_lat = lax.axis_index("lon"), lax.axis_index("lat")
    me = my_lon * n_lat + my_lat
    width = got_innov.shape[-1]
    span = GROUP * width
    tall = lat_cells + 2 * EDGE
    low, high = EDGE, EDGE + lat_cells
    cuts = [slots] + [(slots - 1) * w // (WAVES - 1) for w in range(WAVES - 1, -1, -1)]
    waves = [(end, first) for first, end in zip(cuts, cuts[1:])]

    lat_up = (my_lon, (my_lat + 1) % n_lat)
    lat_down = (my_lon, (my_lat + n_lat - 1) % n_lat)
    lon_up = ((my_lon + 1) % n_lon, my_lat)
    lon_down = ((my_lon + n_lon - 1) % n_lon, my_lat)

    barrier = pltpu.get_barrier_semaphore()

    @pl.loop(1, devices)
    def _(k):
        to = (me + k) % devices
        pl.semaphore_signal(barrier, inc=1, device_id=(to // n_lat, to % n_lat), device_id_type=MESH)

    own_a = pltpu.make_async_copy(innov_ref.at[:, me], got_innov.at[:, 0], own_sem.at[0])
    own_b = pltpu.make_async_copy(meta_ref.at[me], got_meta.at[0], own_sem.at[1])
    own_a.start()
    own_b.start()
    wind[0:LEV, low:high, 0:lon_cells] = 0.5 * u_ref[...]
    wind[LEV : 2 * LEV, low:high, 0:lon_cells] = 0.5 * v_ref[...]
    pl.semaphore_wait(barrier, devices - 1)

    def lat_pair(buffer, send, recv):
        down = pltpu.make_async_remote_copy(
            src_ref=buffer.at[:, low : low + EDGE, 0:lon_cells],
            dst_ref=buffer.at[:, high : high + EDGE, 0:lon_cells],
            send_sem=send.at[0], recv_sem=recv.at[0], device_id=lat_down, device_id_type=MESH,
        )
        up = pltpu.make_async_remote_copy(
            src_ref=buffer.at[:, high - EDGE : high, 0:lon_cells],
            dst_ref=buffer.at[:, 0:low, 0:lon_cells],
            send_sem=send.at[1], recv_sem=recv.at[1], device_id=lat_up, device_id_type=MESH,
        )
        return down, up

    def lon_pair(send_buf, got_buf, send, recv):
        down = pltpu.make_async_remote_copy(
            src_ref=send_buf.at[0], dst_ref=got_buf.at[0],
            send_sem=send.at[0], recv_sem=recv.at[0], device_id=lon_down, device_id_type=MESH,
        )
        up = pltpu.make_async_remote_copy(
            src_ref=send_buf.at[1], dst_ref=got_buf.at[1],
            send_sem=send.at[1], recv_sem=recv.at[1], device_id=lon_up, device_id_type=MESH,
        )
        return down, up

    lane = lax.broadcasted_iota(jnp.int32, (tall, lon_cells), 1)

    def pack(source, count, target):
        first = jnp.zeros((tall, lon_cells), jnp.float32)
        last = first
        for c in range(count):
            body = source[c, :, 0:lon_cells]
            here = (lane >= EDGE * c) & (lane < EDGE * (c + 1))
            a = body if c == 0 else pltpu.roll(body, EDGE * c, 1)
            shift = (EDGE * (c + 1)) % lon_cells
            b = body if shift == 0 else pltpu.roll(body, shift, 1)
            first = jnp.where(here, a, first)
            last = jnp.where(here, b, last)
        target[0] = first
        target[1] = last

    def unpack(got, count, target):
        after, before = got[0], got[1]
        for c in range(count):
            back = (lon_cells - EDGE * c) % lon_cells
            a = after if back == 0 else pltpu.roll(after, back, 1)
            shift = (lon_cells - EDGE - EDGE * c) % lon_cells
            b = before if shift == 0 else pltpu.roll(before, shift, 1)
            target[c, :, lon_cells : 2 * lon_cells] = jnp.where(lane < EDGE, a, b)

    def field_lat(s):
        return lat_pair(field.at[s], flat_send.at[s], flat_recv.at[s])

    def field_lon(s):
        return lon_pair(lon_send.at[s], lon_got.at[s], flon_send.at[s], flon_recv.at[s])

    def wave(w, k, to):
        first, end = waves[w]
        return pltpu.make_async_remote_copy(
            src_ref=innov_ref.at[first:end, to], dst_ref=got_innov.at[first:end, k],
            send_sem=innov_send.at[w], recv_sem=innov_recv.at[w],
            device_id=(to // n_lat, to % n_lat), device_id_type=MESH,
        )

    def wave_total(w):
        first, end = waves[w]
        whole = got_innov.at[first:end, 1:devices]
        return pltpu.make_async_remote_copy(
            src_ref=whole, dst_ref=whole,
            send_sem=innov_send.at[w], recv_sem=innov_recv.at[w], device_id=lat_up, device_id_type=MESH,
        )

    def meta_copy(k, to):
        return pltpu.make_async_remote_copy(
            src_ref=meta_ref.at[to], dst_ref=got_meta.at[k],
            send_sem=meta_send.at[0], recv_sem=meta_recv.at[0],
            device_id=(to // n_lat, to % n_lat), device_id_type=MESH,
        )

    def meta_total():
        whole = got_meta.at[1:devices]
        return pltpu.make_async_remote_copy(
            src_ref=whole, dst_ref=whole,
            send_sem=meta_send.at[0], recv_sem=meta_recv.at[0], device_id=lat_up, device_id_type=MESH,
        )

    wind_lat = lat_pair(wind, wlat_send, wlat_recv)
    wind_lon = lon_pair(wind_send, wind_got, wlon_send, wlon_recv)
    for copy in wind_lat:
        copy.start()

    @pl.loop(1, devices)
    def _(k):
        to = (me + k) % devices
        meta_copy(k, to).start()
        wave(0, k, to).start()

    for w in range(1, len(waves)):

        @pl.loop(1, devices)
        def _(k):
            wave(w, k, (me + k) % devices).start()

    own_a.wait()
    own_b.wait()
    for copy in wind_lat:
        copy.wait()
    pack(wind, 2 * LEV, wind_send)
    for copy in wind_lon:
        copy.start()

    across = lon_cells // TILE
    tile_id = lax.broadcasted_iota(jnp.int32, (TILE, span), 0).astype(jnp.float32)
    lane_group = lax.broadcasted_iota(jnp.int32, (CH, lon_cells), 1) // TILE
    contract = (((1,), (1,)), ((), ()))
    row_at = lax.broadcasted_iota(jnp.int32, (tall, 2 * lon_cells), 0)
    first_row = jnp.where(my_lat == 0, low, 0)
    last_row = jnp.where(my_lat == n_lat - 1, high, tall)
    inside = (row_at >= first_row) & (row_at < last_row)

    def stepped(older, channels):
        below = field[older, 0]
        totals = [mix_ref[0, c] * below for c in channels]
        for d in range(1, CH):
            below = field[older, d]
            totals = [total + mix_ref[d, c] * below for c, total in zip(channels, totals)]
        level = channels[0] % LEV
        half_u, half_v = wind[level], wind[LEV + level]
        results = []
        for total in totals:
            total = jnp.where(inside, total, 0.0)
            eastward = half_u * total
            northward = half_v * total
            near = KAPPA * total
            results.append(
                (1.0 - 4.0 * KAPPA) * total
                + pltpu.roll(near + eastward, 2 * lon_cells - 1, 1)
                + pltpu.roll(near - eastward, 1, 1)
                + pltpu.roll(near + northward, tall - 1, 0)
                + pltpu.roll(near - northward, 1, 0)
            )
        return results

    def same_level(i):
        first = (i // LEV) * LEV * SIDE + i % LEV
        return [first + LEV * j for j in range(SIDE)]

    def take_meta():
        meta_total().wait_recv()

        @pl.loop(0, devices // GROUP)
        def _(g):
            for i in range(GROUP):
                numbers = got_meta[g * GROUP + i].astype(jnp.float32)
                for s in range(slots):
                    rows_buf[s, g, 0:4, i * width : (i + 1) * width] = numbers[4 * s : 4 * s + 4]

    def gather_slot(s):
        acc[...] = jnp.zeros(acc.shape, jnp.float32)

        @pl.loop(0, devices // GROUP)
        def _(g):
            values = jnp.concatenate(
                [got_innov[s, g * GROUP + i] for i in range(GROUP)], axis=1
            )
            frac_y, frac_x = rows_buf[s, g, 0:1], rows_buf[s, g, 1:2]
            cell, block = rows_buf[s, g, 2:3], rows_buf[s, g, 3:4]
            row = jnp.floor(cell * (1.0 / TILE))
            col = cell - TILE * row
            in_rows = jnp.where(tile_id == row, 1.0 - frac_y, jnp.where(tile_id == row + 1.0, frac_y, 0.0))
            in_cols = jnp.where(tile_id == col, 1.0 - frac_x, jnp.where(tile_id == col + 1.0, frac_x, 0.0))
            heads, tails = [], []
            for r in range(TILE):
                weight = in_rows[r : r + 1] * in_cols
                head = weight.astype(jnp.bfloat16)
                heads.append(head)
                tails.append((weight - head.astype(jnp.float32)).astype(jnp.bfloat16))
            weights = jnp.concatenate(heads + tails, axis=0)
            placed = []
            for b in range(lat_cells // TILE * across):
                here = jnp.broadcast_to(jnp.where(block == float(b), 1.0, 0.0), (CH, span)).astype(jnp.bfloat16)
                placed.append(values * here)
            placed = jnp.concatenate(placed, axis=0)
            both = lax.dot_general(weights, placed, contract, preferred_element_type=jnp.float32)
            acc[...] += both[: TILE * TILE] + both[TILE * TILE :]

        tiles = jnp.transpose(acc[...])
        strips = []
        for down in range(lat_cells // TILE):
            for half in range(TILE // across):
                x = []
                for i in range(across):
                    b = down * across + i
                    x.append(tiles[b * CH : (b + 1) * CH, half * lon_cells : (half + 1) * lon_cells])
                apart = 1
                while apart < across:
                    moved = list(x)
                    for i in range(across):
                        if i & apart == 0:
                            j = i + apart
                            moved[i] = jnp.where(lane_group & apart == 0, x[i], pltpu.roll(x[j], TILE * apart, 1))
                            moved[j] = jnp.where(
                                lane_group & apart == 0, pltpu.roll(x[i], lon_cells - TILE * apart, 1), x[j]
                            )
                    x = moved
                    apart *= 2
                strips += x
        whole = jnp.stack(strips, axis=0)
        field[s, :, low:high, 0:lon_cells] = jnp.swapaxes(whole, 0, 1)

    def settle(s):
        for copy in field_lon(s):
            copy.wait_recv()
        unpack(lon_got.at[s], CH, field.at[s])

        @pl.when(s < slots - 1)
        def _():
            @pl.loop(0, CH // SIDE)
            def _(i):
                channels = same_level(i)
                news = [new + field[s, c] for c, new in zip(channels, stepped(s + 1, channels))]
                for c, new in zip(channels, news):
                    field[s, c] = new

    take_meta()

    @pl.loop(0, slots)
    def _(n):
        s = slots - 1 - n
        for w, (_, end) in enumerate(waves):

            @pl.when(s == end - 1)
            def _():
                wave_total(w).wait_recv()

        gather_slot(s)

        @pl.when(s > 0)
        def _():
            for copy in field_lat(s):
                copy.start()

        @pl.when(n >= 1)
        def _():
            for copy in field_lat(s + 1):
                copy.wait()
            pack(field.at[s + 1], CH, lon_send.at[s + 1])
            for copy in field_lon(s + 1):
                copy.start()

        @pl.when(n == 1)
        def _():
            for copy in wind_lon:
                copy.wait()
            unpack(wind_got, 2 * LEV, wind)

        @pl.when(n >= 2)
        def _():
            settle(s + 2)

    settle(1)

    @pl.loop(0, CH // SIDE)
    def _(i):
        channels = same_level(i)
        for c, new in zip(channels, stepped(1, channels)):
            out_ref[c] = new[low:high, 0:lon_cells] + field[0, c, low:high, 0:lon_cells]

    @pl.loop(1, slots)
    def _(s):
        for copy in field_lon(s):
            copy.wait_send()

    for w in range(len(waves)):
        wave_total(w).wait_send()
    meta_total().wait_send()


def shards(n_lon, n_lat, innovations, fractions, cell_index, counts, blocks, u_wind, v_wind, channel_mix):
    slots, devices, channels, width = innovations.shape
    lat_cells, lon_cells = u_wind.shape[1:]
    tiles = counts.shape[2]
    per_tile = width // tiles
    within = lax.broadcasted_iota(jnp.int32, (1, 1, tiles, per_tile), 3)
    live = within < counts[..., None]
    block = jnp.where(live, blocks[..., None], -1).reshape(slots, devices, width)
    places = jnp.stack([cell_index, block], axis=2).astype(jnp.bfloat16)
    meta = jnp.concatenate([fractions, places], axis=2)
    meta = jnp.transpose(meta, (1, 0, 2, 3)).reshape(devices, 4 * slots, width)
    meta_rows = -(-4 * slots // 16) * 16
    meta = jnp.pad(meta, ((0, 0), (0, meta_rows - 4 * slots), (0, 0)))

    tall, wide = lat_cells + 2 * EDGE, 2 * lon_cells
    f32, bf16, dma = jnp.float32, jnp.bfloat16, pltpu.SemaphoreType.DMA
    vmem = pl.BlockSpec(memory_space=pltpu.VMEM)
    out = pl.pallas_call(
        functools.partial(kernel, n_lon, n_lat, slots, lat_cells, lon_cells),
        out_shape=jax.ShapeDtypeStruct((CH, lat_cells, lon_cells), f32),
        in_specs=[
            pl.BlockSpec(memory_space=pltpu.SMEM),
            pl.BlockSpec(memory_space=pl.ANY),
            pl.BlockSpec(memory_space=pl.ANY),
            vmem,
            vmem,
        ],
        out_specs=vmem,
        scratch_shapes=[
            pltpu.VMEM((slots, devices, channels, width), bf16),
            pltpu.VMEM((devices, meta_rows, width), bf16),
            pltpu.VMEM((slots, devices // GROUP, 8, GROUP * width), f32),
            pltpu.VMEM((TILE * TILE, CH * lat_cells * lon_cells // TILE**2), f32),
            pltpu.VMEM((slots, CH, tall, wide), f32),
            pltpu.VMEM((2 * LEV, tall, wide), f32),
            pltpu.VMEM((2, tall, lon_cells), f32),
            pltpu.VMEM((2, tall, lon_cells), f32),
            pltpu.VMEM((slots, 2, tall, lon_cells), f32),
            pltpu.VMEM((slots, 2, tall, lon_cells), f32),
            dma((2,)),
            dma((WAVES,)),
            dma((WAVES,)),
            dma((1,)),
            dma((1,)),
            dma((2,)),
            dma((2,)),
            dma((2,)),
            dma((2,)),
            dma((slots, 2)),
            dma((slots, 2)),
            dma((slots, 2)),
            dma((slots, 2)),
        ],
        compiler_params=pltpu.CompilerParams(
            collective_id=0, has_side_effects=True, vmem_limit_bytes=48 * 1024 * 1024
        ),
    )(channel_mix, innovations, meta, u_wind, v_wind)
    return out.reshape(VARS, LEV, lat_cells, lon_cells)


def solution(mesh):
    in_specs = (
        P(None, ("lon", "lat"), None, None),
        P(None, ("lon", "lat"), None, None),
        P(None, ("lon", "lat"), None),
        P(None, ("lon", "lat"), None),
        P(None, ("lon", "lat"), None),
        P(None, "lat", "lon"),
        P(None, "lat", "lon"),
        P(),
    )
    out_specs = P(None, None, "lat", "lon")
    body = functools.partial(shards, mesh.shape["lon"], mesh.shape["lat"])
    return jax.shard_map(body, mesh=mesh, in_specs=in_specs, out_specs=out_specs, check_vma=False)
```

```python
import functools

import jax
import jax.numpy as jnp
from jax import lax
from jax.experimental import pallas as pl
from jax.experimental.pallas import tpu as pltpu
from jax.sharding import PartitionSpec as P

VARS = 4
LEV = 4
CH = 16
TILE = 16
KAPPA = 0.125
EDGE = 8
GROUP = 8
SIDE = 2
WAVE = 2
MESH = pl.DeviceIdType.MESH


def kernel(
    n_lon, n_lat, slots, lat_cells, lon_cells,
    mix_ref, innov_ref, meta_ref, u_ref, v_ref, out_ref,
    got_innov, got_meta, rows_buf, acc, field, wind, wind_send, wind_got, lon_send, lon_got,
    own_sem, innov_send, innov_recv, meta_send, meta_recv,
    wlat_send, wlat_recv, wlon_send, wlon_recv, flat_send, flat_recv, flon_send, flon_recv,
):
    devices = n_lon * n_lat
    my_lon, my_lat = lax.axis_index("lon"), lax.axis_index("lat")
    me = my_lon * n_lat + my_lat
    width = got_innov.shape[-1]
    span = GROUP * width
    tall = lat_cells + 2 * EDGE
    low, high = EDGE, EDGE + lat_cells
    waves = [(slots - 1, slots)]
    while waves[-1][0] > 0:
        end = waves[-1][0]
        waves.append((max(end - WAVE, 0), end))
    metas = got_meta.shape[0]

    lat_up = (my_lon, (my_lat + 1) % n_lat)
    lat_down = (my_lon, (my_lat + n_lat - 1) % n_lat)
    lon_up = ((my_lon + 1) % n_lon, my_lat)
    lon_down = ((my_lon + n_lon - 1) % n_lon, my_lat)

    barrier = pltpu.get_barrier_semaphore()

    @pl.loop(1, devices)
    def _(k):
        to = (me + k) % devices
        pl.semaphore_signal(barrier, inc=1, device_id=(to // n_lat, to % n_lat), device_id_type=MESH)

    own_a = pltpu.make_async_copy(innov_ref.at[:, me], got_innov.at[:, 0], own_sem.at[0])
    own_b = pltpu.make_async_copy(meta_ref.at[:, me], got_meta.at[:, 0], own_sem.at[1])
    own_a.start()
    own_b.start()
    wind[0:LEV, low:high, 0:lon_cells] = 0.5 * u_ref[...]
    wind[LEV : 2 * LEV, low:high, 0:lon_cells] = 0.5 * v_ref[...]
    pl.semaphore_wait(barrier, devices - 1)

    def lat_pair(buffer, send, recv):
        down = pltpu.make_async_remote_copy(
            src_ref=buffer.at[:, low : low + EDGE, 0:lon_cells],
            dst_ref=buffer.at[:, high : high + EDGE, 0:lon_cells],
            send_sem=send.at[0], recv_sem=recv.at[0], device_id=lat_down, device_id_type=MESH,
        )
        up = pltpu.make_async_remote_copy(
            src_ref=buffer.at[:, high - EDGE : high, 0:lon_cells],
            dst_ref=buffer.at[:, 0:low, 0:lon_cells],
            send_sem=send.at[1], recv_sem=recv.at[1], device_id=lat_up, device_id_type=MESH,
        )
        return down, up

    def lon_pair(send_buf, got_buf, send, recv):
        down = pltpu.make_async_remote_copy(
            src_ref=send_buf.at[0], dst_ref=got_buf.at[0],
            send_sem=send.at[0], recv_sem=recv.at[0], device_id=lon_down, device_id_type=MESH,
        )
        up = pltpu.make_async_remote_copy(
            src_ref=send_buf.at[1], dst_ref=got_buf.at[1],
            send_sem=send.at[1], recv_sem=recv.at[1], device_id=lon_up, device_id_type=MESH,
        )
        return down, up

    lane = lax.broadcasted_iota(jnp.int32, (tall, lon_cells), 1)

    def pack(source, count, target):
        first = jnp.zeros((tall, lon_cells), jnp.float32)
        last = first
        for c in range(count):
            body = source[c, :, 0:lon_cells]
            here = (lane >= EDGE * c) & (lane < EDGE * (c + 1))
            a = body if c == 0 else pltpu.roll(body, EDGE * c, 1)
            shift = (EDGE * (c + 1)) % lon_cells
            b = body if shift == 0 else pltpu.roll(body, shift, 1)
            first = jnp.where(here, a, first)
            last = jnp.where(here, b, last)
        target[0] = first
        target[1] = last

    def unpack(got, count, target):
        after, before = got[0], got[1]
        for c in range(count):
            back = (lon_cells - EDGE * c) % lon_cells
            a = after if back == 0 else pltpu.roll(after, back, 1)
            shift = (lon_cells - EDGE - EDGE * c) % lon_cells
            b = before if shift == 0 else pltpu.roll(before, shift, 1)
            target[c, :, lon_cells : 2 * lon_cells] = jnp.where(lane < EDGE, a, b)

    def field_lat(s):
        return lat_pair(field.at[s], flat_send.at[s], flat_recv.at[s])

    def field_lon(s):
        return lon_pair(lon_send.at[s], lon_got.at[s], flon_send.at[s], flon_recv.at[s])

    def wave(w, k, to):
        first, end = waves[w]
        return pltpu.make_async_remote_copy(
            src_ref=innov_ref.at[first:end, to], dst_ref=got_innov.at[first:end, k],
            send_sem=innov_send.at[w], recv_sem=innov_recv.at[w],
            device_id=(to // n_lat, to % n_lat), device_id_type=MESH,
        )

    def wave_total(w):
        first, end = waves[w]
        whole = got_innov.at[first:end, 1:devices]
        return pltpu.make_async_remote_copy(
            src_ref=whole, dst_ref=whole,
            send_sem=innov_send.at[w], recv_sem=innov_recv.at[w], device_id=lat_up, device_id_type=MESH,
        )

    def meta_copy(m, k, to):
        return pltpu.make_async_remote_copy(
            src_ref=meta_ref.at[m, to], dst_ref=got_meta.at[m, k],
            send_sem=meta_send.at[m], recv_sem=meta_recv.at[m],
            device_id=(to // n_lat, to % n_lat), device_id_type=MESH,
        )

    def meta_total(m):
        whole = got_meta.at[m, 1:devices]
        return pltpu.make_async_remote_copy(
            src_ref=whole, dst_ref=whole,
            send_sem=meta_send.at[m], recv_sem=meta_recv.at[m], device_id=lat_up, device_id_type=MESH,
        )

    wind_lat = lat_pair(wind, wlat_send, wlat_recv)
    wind_lon = lon_pair(wind_send, wind_got, wlon_send, wlon_recv)
    for copy in wind_lat:
        copy.start()

    def send_wave(w):
        @pl.loop(1, devices)
        def _(k):
            to = (me + k) % devices
            if w == 0:
                meta_copy(0, k, to).start()
            if w == 2:
                for m in range(1, metas):
                    meta_copy(m, k, to).start()
            wave(w, k, to).start()

    send_wave(0)
    send_wave(1)
    own_a.wait()
    own_b.wait()
    for copy in wind_lat:
        copy.wait()
    pack(wind, 2 * LEV, wind_send)
    for copy in wind_lon:
        copy.start()

    across = lon_cells // TILE
    tile_id = lax.broadcasted_iota(jnp.int32, (TILE, span), 0).astype(jnp.float32)
    lane_group = lax.broadcasted_iota(jnp.int32, (CH, lon_cells), 1) // TILE
    contract = (((1,), (1,)), ((), ()))
    row_at = lax.broadcasted_iota(jnp.int32, (tall, 2 * lon_cells), 0)
    first_row = jnp.where(my_lat == 0, low, 0)
    last_row = jnp.where(my_lat == n_lat - 1, high, tall)
    inside = (row_at >= first_row) & (row_at < last_row)

    def stepped(older, channels):
        below = field[older, 0]
        totals = [mix_ref[0, c] * below for c in channels]
        for d in range(1, CH):
            below = field[older, d]
            totals = [total + mix_ref[d, c] * below for c, total in zip(channels, totals)]
        level = channels[0] % LEV
        half_u, half_v = wind[level], wind[LEV + level]
        results = []
        for total in totals:
            total = jnp.where(inside, total, 0.0)
            eastward = half_u * total
            northward = half_v * total
            near = KAPPA * total
            results.append(
                (1.0 - 4.0 * KAPPA) * total
                + pltpu.roll(near + eastward, 2 * lon_cells - 1, 1)
                + pltpu.roll(near - eastward, 1, 1)
                + pltpu.roll(near + northward, tall - 1, 0)
                + pltpu.roll(near - northward, 1, 0)
            )
        return results

    def same_level(i):
        first = (i // LEV) * LEV * SIDE + i % LEV
        return [first + LEV * j for j in range(SIDE)]

    def take_meta(m):
        meta_total(m).wait_recv()

        @pl.loop(0, devices // GROUP)
        def _(g):
            for i in range(GROUP):
                numbers = got_meta[m, g * GROUP + i].astype(jnp.float32)
                for j in range(4):
                    s = slots - 1 - (4 * m + j)
                    if s >= 0:
                        rows_buf[s, g, 0:4, i * width : (i + 1) * width] = numbers[4 * j : 4 * j + 4]

    def gather_slot(s):
        acc[...] = jnp.zeros(acc.shape, jnp.float32)

        @pl.loop(0, devices // GROUP)
        def _(g):
            values = jnp.concatenate(
                [got_innov[s, g * GROUP + i] for i in range(GROUP)], axis=1
            )
            frac_y, frac_x = rows_buf[s, g, 0:1], rows_buf[s, g, 1:2]
            cell, block = rows_buf[s, g, 2:3], rows_buf[s, g, 3:4]
            row = jnp.floor(cell * (1.0 / TILE))
            col = cell - TILE * row
            in_rows = jnp.where(tile_id == row, 1.0 - frac_y, jnp.where(tile_id == row + 1.0, frac_y, 0.0))
            in_cols = jnp.where(tile_id == col, 1.0 - frac_x, jnp.where(tile_id == col + 1.0, frac_x, 0.0))
            heads, tails = [], []
            for r in range(TILE):
                weight = in_rows[r : r + 1] * in_cols
                head = weight.astype(jnp.bfloat16)
                heads.append(head)
                tails.append((weight - head.astype(jnp.float32)).astype(jnp.bfloat16))
            weights = jnp.concatenate(heads + tails, axis=0)
            placed = []
            for b in range(lat_cells // TILE * across):
                here = jnp.broadcast_to(jnp.where(block == float(b), 1.0, 0.0), (CH, span)).astype(jnp.bfloat16)
                placed.append(values * here)
            placed = jnp.concatenate(placed, axis=0)
            both = lax.dot_general(weights, placed, contract, preferred_element_type=jnp.float32)
            acc[...] += both[: TILE * TILE] + both[TILE * TILE :]

        tiles = jnp.transpose(acc[...])
        strips = []
        for down in range(lat_cells // TILE):
            for half in range(TILE // across):
                x = []
                for i in range(across):
                    b = down * across + i
                    x.append(tiles[b * CH : (b + 1) * CH, half * lon_cells : (half + 1) * lon_cells])
                apart = 1
                while apart < across:
                    moved = list(x)
                    for i in range(across):
                        if i & apart == 0:
                            j = i + apart
                            moved[i] = jnp.where(lane_group & apart == 0, x[i], pltpu.roll(x[j], TILE * apart, 1))
                            moved[j] = jnp.where(
                                lane_group & apart == 0, pltpu.roll(x[i], lon_cells - TILE * apart, 1), x[j]
                            )
                    x = moved
                    apart *= 2
                strips += x
        whole = jnp.stack(strips, axis=0)
        field[s, :, low:high, 0:lon_cells] = jnp.swapaxes(whole, 0, 1)

    def settle(s):
        for copy in field_lon(s):
            copy.wait_recv()
        unpack(lon_got.at[s], CH, field.at[s])

        @pl.when(s < slots - 1)
        def _():
            @pl.loop(0, CH // SIDE)
            def _(i):
                channels = same_level(i)
                news = [new + field[s, c] for c, new in zip(channels, stepped(s + 1, channels))]
                for c, new in zip(channels, news):
                    field[s, c] = new

    @pl.loop(0, slots)
    def _(n):
        s = slots - 1 - n
        for w, (_, end) in enumerate(waves):

            @pl.when(s == end - 1)
            def _():
                wave_total(w).wait_recv()

        for m in range(metas):

            @pl.when(n == 4 * m)
            def _():
                take_meta(m)

        gather_slot(s)

        @pl.when(s > 0)
        def _():
            for copy in field_lat(s):
                copy.start()

        @pl.when(n >= 1)
        def _():
            for copy in field_lat(s + 1):
                copy.wait()
            pack(field.at[s + 1], CH, lon_send.at[s + 1])
            for copy in field_lon(s + 1):
                copy.start()

        for w in range(2, len(waves)):

            @pl.when(n == WAVE * w - 3)
            def _():
                send_wave(w)

        @pl.when(n == 1)
        def _():
            for copy in wind_lon:
                copy.wait()
            unpack(wind_got, 2 * LEV, wind)

        @pl.when(n >= 2)
        def _():
            settle(s + 2)

    settle(1)

    @pl.loop(0, CH // SIDE)
    def _(i):
        channels = same_level(i)
        for c, new in zip(channels, stepped(1, channels)):
            out_ref[c] = new[low:high, 0:lon_cells] + field[0, c, low:high, 0:lon_cells]

    @pl.loop(1, slots)
    def _(s):
        for copy in field_lon(s):
            copy.wait_send()

    for w in range(len(waves)):
        wave_total(w).wait_send()
    for m in range(metas):
        meta_total(m).wait_send()


def shards(n_lon, n_lat, innovations, fractions, cell_index, counts, blocks, u_wind, v_wind, channel_mix):
    slots, devices, channels, width = innovations.shape
    lat_cells, lon_cells = u_wind.shape[1:]
    tiles = counts.shape[2]
    per_tile = width // tiles
    within = lax.broadcasted_iota(jnp.int32, (1, 1, tiles, per_tile), 3)
    live = within < counts[..., None]
    block = jnp.where(live, blocks[..., None], -1).reshape(slots, devices, width)
    places = jnp.stack([cell_index, block], axis=2).astype(jnp.bfloat16)
    meta = jnp.concatenate([fractions, places], axis=2)
    metas, waves = -(-slots // 4), 1 - (1 - slots) // WAVE
    meta = jnp.pad(meta[::-1], ((0, 4 * metas - slots), (0, 0), (0, 0), (0, 0)))
    meta = meta.reshape(metas, 4, devices, 4, width)
    meta = jnp.transpose(meta, (0, 2, 1, 3, 4)).reshape(metas, devices, 16, width)

    tall, wide = lat_cells + 2 * EDGE, 2 * lon_cells
    f32, bf16, dma = jnp.float32, jnp.bfloat16, pltpu.SemaphoreType.DMA
    vmem = pl.BlockSpec(memory_space=pltpu.VMEM)
    out = pl.pallas_call(
        functools.partial(kernel, n_lon, n_lat, slots, lat_cells, lon_cells),
        out_shape=jax.ShapeDtypeStruct((CH, lat_cells, lon_cells), f32),
        in_specs=[
            pl.BlockSpec(memory_space=pltpu.SMEM),
            pl.BlockSpec(memory_space=pl.ANY),
            pl.BlockSpec(memory_space=pl.ANY),
            vmem,
            vmem,
        ],
        out_specs=vmem,
        scratch_shapes=[
            pltpu.VMEM((slots, devices, channels, width), bf16),
            pltpu.VMEM((metas, devices, 16, width), bf16),
            pltpu.VMEM((slots, devices // GROUP, 8, GROUP * width), f32),
            pltpu.VMEM((TILE * TILE, CH * lat_cells * lon_cells // TILE**2), f32),
            pltpu.VMEM((slots, CH, tall, wide), f32),
            pltpu.VMEM((2 * LEV, tall, wide), f32),
            pltpu.VMEM((2, tall, lon_cells), f32),
            pltpu.VMEM((2, tall, lon_cells), f32),
            pltpu.VMEM((slots, 2, tall, lon_cells), f32),
            pltpu.VMEM((slots, 2, tall, lon_cells), f32),
            dma((2,)),
            dma((waves,)),
            dma((waves,)),
            dma((metas,)),
            dma((metas,)),
            dma((2,)),
            dma((2,)),
            dma((2,)),
            dma((2,)),
            dma((slots, 2)),
            dma((slots, 2)),
            dma((slots, 2)),
            dma((slots, 2)),
        ],
        compiler_params=pltpu.CompilerParams(
            collective_id=0, has_side_effects=True, vmem_limit_bytes=48 * 1024 * 1024
        ),
    )(channel_mix, innovations, meta, u_wind, v_wind)
    return out.reshape(VARS, LEV, lat_cells, lon_cells)


def solution(mesh):
    in_specs = (
        P(None, ("lon", "lat"), None, None),
        P(None, ("lon", "lat"), None, None),
        P(None, ("lon", "lat"), None),
        P(None, ("lon", "lat"), None),
        P(None, ("lon", "lat"), None),
        P(None, "lat", "lon"),
        P(None, "lat", "lon"),
        P(),
    )
    out_specs = P(None, None, "lat", "lon")
    body = functools.partial(shards, mesh.shape["lon"], mesh.shape["lat"])
    return jax.shard_map(body, mesh=mesh, in_specs=in_specs, out_specs=out_specs, check_vma=False)
```

```python
import functools

import jax
import jax.numpy as jnp
from jax import lax
from jax.experimental import pallas as pl
from jax.experimental.pallas import tpu as pltpu
from jax.sharding import PartitionSpec as P

VARS = 4
LEV = 4
CH = 16
TILE = 16
KAPPA = 0.125
EDGE = 8
GROUP = 8
SIDE = 4
WAVE = 2
MESH = pl.DeviceIdType.MESH


def kernel(
    n_lon, n_lat, slots, lat_cells, lon_cells,
    mix_ref, innov_ref, meta_ref, u_ref, v_ref, out_ref,
    got_innov, got_meta, rows_buf, acc, field, wind, wind_send, wind_got, lon_send, lon_got,
    own_sem, innov_send, innov_recv, meta_send, meta_recv,
    wlat_send, wlat_recv, wlon_send, wlon_recv, flat_send, flat_recv, flon_send, flon_recv,
):
    devices = n_lon * n_lat
    my_lon, my_lat = lax.axis_index("lon"), lax.axis_index("lat")
    me = my_lon * n_lat + my_lat
    width = got_innov.shape[-1]
    span = GROUP * width
    tall = lat_cells + 2 * EDGE
    low, high = EDGE, EDGE + lat_cells
    waves = [(slots - 1, slots)]
    while waves[-1][0] > 0:
        end = waves[-1][0]
        waves.append((max(end - WAVE, 0), end))
    metas = got_meta.shape[0]

    lat_up = (my_lon, (my_lat + 1) % n_lat)
    lat_down = (my_lon, (my_lat + n_lat - 1) % n_lat)
    lon_up = ((my_lon + 1) % n_lon, my_lat)
    lon_down = ((my_lon + n_lon - 1) % n_lon, my_lat)

    barrier = pltpu.get_barrier_semaphore()

    @pl.loop(1, devices)
    def _(k):
        to = (me + k) % devices
        pl.semaphore_signal(barrier, inc=1, device_id=(to // n_lat, to % n_lat), device_id_type=MESH)

    own_a = pltpu.make_async_copy(innov_ref.at[:, me], got_innov.at[:, 0], own_sem.at[0])
    own_b = pltpu.make_async_copy(meta_ref.at[:, me], got_meta.at[:, 0], own_sem.at[1])
    own_a.start()
    own_b.start()
    wind[0:LEV, low:high, 0:lon_cells] = 0.5 * u_ref[...]
    wind[LEV : 2 * LEV, low:high, 0:lon_cells] = 0.5 * v_ref[...]
    pl.semaphore_wait(barrier, devices - 1)

    def lat_pair(buffer, send, recv):
        down = pltpu.make_async_remote_copy(
            src_ref=buffer.at[:, low : low + EDGE, 0:lon_cells],
            dst_ref=buffer.at[:, high : high + EDGE, 0:lon_cells],
            send_sem=send.at[0], recv_sem=recv.at[0], device_id=lat_down, device_id_type=MESH,
        )
        up = pltpu.make_async_remote_copy(
            src_ref=buffer.at[:, high - EDGE : high, 0:lon_cells],
            dst_ref=buffer.at[:, 0:low, 0:lon_cells],
            send_sem=send.at[1], recv_sem=recv.at[1], device_id=lat_up, device_id_type=MESH,
        )
        return down, up

    def lon_pair(send_buf, got_buf, send, recv):
        down = pltpu.make_async_remote_copy(
            src_ref=send_buf.at[0], dst_ref=got_buf.at[0],
            send_sem=send.at[0], recv_sem=recv.at[0], device_id=lon_down, device_id_type=MESH,
        )
        up = pltpu.make_async_remote_copy(
            src_ref=send_buf.at[1], dst_ref=got_buf.at[1],
            send_sem=send.at[1], recv_sem=recv.at[1], device_id=lon_up, device_id_type=MESH,
        )
        return down, up

    lane = lax.broadcasted_iota(jnp.int32, (tall, lon_cells), 1)

    def pack(source, count, target):
        first = jnp.zeros((tall, lon_cells), jnp.float32)
        last = first
        for c in range(count):
            body = source[c, :, 0:lon_cells]
            here = (lane >= EDGE * c) & (lane < EDGE * (c + 1))
            a = body if c == 0 else pltpu.roll(body, EDGE * c, 1)
            shift = (EDGE * (c + 1)) % lon_cells
            b = body if shift == 0 else pltpu.roll(body, shift, 1)
            first = jnp.where(here, a, first)
            last = jnp.where(here, b, last)
        target[0] = first
        target[1] = last

    def unpack(got, count, target):
        after, before = got[0], got[1]
        for c in range(count):
            back = (lon_cells - EDGE * c) % lon_cells
            a = after if back == 0 else pltpu.roll(after, back, 1)
            shift = (lon_cells - EDGE - EDGE * c) % lon_cells
            b = before if shift == 0 else pltpu.roll(before, shift, 1)
            target[c, :, lon_cells : 2 * lon_cells] = jnp.where(lane < EDGE, a, b)

    def field_lat(s):
        return lat_pair(field.at[s], flat_send.at[s], flat_recv.at[s])

    def field_lon(s):
        return lon_pair(lon_send.at[s], lon_got.at[s], flon_send.at[s], flon_recv.at[s])

    def wave(w, k, to):
        first, end = waves[w]
        return pltpu.make_async_remote_copy(
            src_ref=innov_ref.at[first:end, to], dst_ref=got_innov.at[first:end, k],
            send_sem=innov_send.at[w], recv_sem=innov_recv.at[w],
            device_id=(to // n_lat, to % n_lat), device_id_type=MESH,
        )

    def wave_total(w):
        first, end = waves[w]
        whole = got_innov.at[first:end, 1:devices]
        return pltpu.make_async_remote_copy(
            src_ref=whole, dst_ref=whole,
            send_sem=innov_send.at[w], recv_sem=innov_recv.at[w], device_id=lat_up, device_id_type=MESH,
        )

    def meta_copy(m, k, to):
        return pltpu.make_async_remote_copy(
            src_ref=meta_ref.at[m, to], dst_ref=got_meta.at[m, k],
            send_sem=meta_send.at[m], recv_sem=meta_recv.at[m],
            device_id=(to // n_lat, to % n_lat), device_id_type=MESH,
        )

    def meta_total(m):
        whole = got_meta.at[m, 1:devices]
        return pltpu.make_async_remote_copy(
            src_ref=whole, dst_ref=whole,
            send_sem=meta_send.at[m], recv_sem=meta_recv.at[m], device_id=lat_up, device_id_type=MESH,
        )

    wind_lat = lat_pair(wind, wlat_send, wlat_recv)
    wind_lon = lon_pair(wind_send, wind_got, wlon_send, wlon_recv)
    for copy in wind_lat:
        copy.start()

    def send_wave(w):
        @pl.loop(1, devices)
        def _(k):
            to = (me + k) % devices
            if w == 0:
                meta_copy(0, k, to).start()
            if w == 2:
                for m in range(1, metas):
                    meta_copy(m, k, to).start()
            wave(w, k, to).start()

    send_wave(0)
    send_wave(1)
    own_a.wait()
    own_b.wait()
    for copy in wind_lat:
        copy.wait()
    pack(wind, 2 * LEV, wind_send)
    for copy in wind_lon:
        copy.start()

    across = lon_cells // TILE
    tile_id = lax.broadcasted_iota(jnp.int32, (TILE, span), 0).astype(jnp.float32)
    lane_group = lax.broadcasted_iota(jnp.int32, (CH, lon_cells), 1) // TILE
    contract = (((1,), (1,)), ((), ()))
    row_at = lax.broadcasted_iota(jnp.int32, (tall, 2 * lon_cells), 0)
    first_row = jnp.where(my_lat == 0, low, 0)
    last_row = jnp.where(my_lat == n_lat - 1, high, tall)
    inside = (row_at >= first_row) & (row_at < last_row)

    def stepped(older, channels):
        below = field[older, 0]
        totals = [mix_ref[0, c] * below for c in channels]
        for d in range(1, CH):
            below = field[older, d]
            totals = [total + mix_ref[d, c] * below for c, total in zip(channels, totals)]
        level = channels[0] % LEV
        half_u, half_v = wind[level], wind[LEV + level]
        results = []
        for total in totals:
            total = jnp.where(inside, total, 0.0)
            eastward = half_u * total
            northward = half_v * total
            near = KAPPA * total
            results.append(
                (1.0 - 4.0 * KAPPA) * total
                + pltpu.roll(near + eastward, 2 * lon_cells - 1, 1)
                + pltpu.roll(near - eastward, 1, 1)
                + pltpu.roll(near + northward, tall - 1, 0)
                + pltpu.roll(near - northward, 1, 0)
            )
        return results

    def same_level(i):
        first = (i // LEV) * LEV * SIDE + i % LEV
        return [first + LEV * j for j in range(SIDE)]

    def take_meta(m):
        meta_total(m).wait_recv()

        @pl.loop(0, devices // GROUP)
        def _(g):
            for i in range(GROUP):
                numbers = got_meta[m, g * GROUP + i].astype(jnp.float32)
                for j in range(4):
                    s = slots - 1 - (4 * m + j)
                    if s >= 0:
                        rows_buf[s, g, 0:4, i * width : (i + 1) * width] = numbers[4 * j : 4 * j + 4]

    def gather_slot(s):
        acc[...] = jnp.zeros(acc.shape, jnp.float32)

        @pl.loop(0, devices // GROUP)
        def _(g):
            values = jnp.concatenate(
                [got_innov[s, g * GROUP + i] for i in range(GROUP)], axis=1
            ).astype(jnp.float32)
            frac_y, frac_x = rows_buf[s, g, 0:1], rows_buf[s, g, 1:2]
            cell, block = rows_buf[s, g, 2:3], rows_buf[s, g, 3:4]
            row = jnp.floor(cell * (1.0 / TILE))
            col = cell - TILE * row
            in_rows = jnp.where(tile_id == row, 1.0 - frac_y, jnp.where(tile_id == row + 1.0, frac_y, 0.0))
            in_cols = jnp.where(tile_id == col, 1.0 - frac_x, jnp.where(tile_id == col + 1.0, frac_x, 0.0))
            heads, tails = [], []
            for r in range(TILE):
                weight = in_rows[r : r + 1] * in_cols
                head = weight.astype(jnp.bfloat16)
                heads.append(head)
                tails.append((weight - head.astype(jnp.float32)).astype(jnp.bfloat16))
            weights = jnp.concatenate(heads + tails, axis=0)
            blocks = jnp.broadcast_to(block, (CH, span))
            placed = []
            for b in range(lat_cells // TILE * across):
                placed.append(jnp.where(blocks == float(b), values, 0.0).astype(jnp.bfloat16))
            placed = jnp.concatenate(placed, axis=0)
            both = lax.dot_general(weights, placed, contract, preferred_element_type=jnp.float32)
            acc[...] += both[: TILE * TILE] + both[TILE * TILE :]

        tiles = jnp.transpose(acc[...])
        strips = []
        for down in range(lat_cells // TILE):
            for half in range(TILE // across):
                x = []
                for i in range(across):
                    b = down * across + i
                    x.append(tiles[b * CH : (b + 1) * CH, half * lon_cells : (half + 1) * lon_cells])
                apart = 1
                while apart < across:
                    moved = list(x)
                    for i in range(across):
                        if i & apart == 0:
                            j = i + apart
                            moved[i] = jnp.where(lane_group & apart == 0, x[i], pltpu.roll(x[j], TILE * apart, 1))
                            moved[j] = jnp.where(
                                lane_group & apart == 0, pltpu.roll(x[i], lon_cells - TILE * apart, 1), x[j]
                            )
                    x = moved
                    apart *= 2
                strips += x
        whole = jnp.stack(strips, axis=0)
        field[s, :, low:high, 0:lon_cells] = jnp.swapaxes(whole, 0, 1)

    def settle(s):
        for copy in field_lon(s):
            copy.wait_recv()
        unpack(lon_got.at[s], CH, field.at[s])

        @pl.when(s < slots - 1)
        def _():
            @pl.loop(0, CH // SIDE)
            def _(i):
                channels = same_level(i)
                news = [new + field[s, c] for c, new in zip(channels, stepped(s + 1, channels))]
                for c, new in zip(channels, news):
                    field[s, c] = new

    @pl.loop(0, slots)
    def _(n):
        s = slots - 1 - n
        for w, (_, end) in enumerate(waves):

            @pl.when(s == end - 1)
            def _():
                wave_total(w).wait_recv()

        for m in range(metas):

            @pl.when(n == 4 * m)
            def _():
                take_meta(m)

        gather_slot(s)

        @pl.when(s > 0)
        def _():
            for copy in field_lat(s):
                copy.start()

        @pl.when(n >= 1)
        def _():
            for copy in field_lat(s + 1):
                copy.wait()
            pack(field.at[s + 1], CH, lon_send.at[s + 1])
            for copy in field_lon(s + 1):
                copy.start()

        for w in range(2, len(waves)):

            @pl.when(n == WAVE * w - 4)
            def _():
                send_wave(w)

        @pl.when(n == 1)
        def _():
            for copy in wind_lon:
                copy.wait()
            unpack(wind_got, 2 * LEV, wind)

        @pl.when(n >= 2)
        def _():
            settle(s + 2)

    settle(1)

    @pl.loop(0, CH // SIDE)
    def _(i):
        channels = same_level(i)
        for c, new in zip(channels, stepped(1, channels)):
            out_ref[c] = new[low:high, 0:lon_cells] + field[0, c, low:high, 0:lon_cells]

    @pl.loop(1, slots)
    def _(s):
        for copy in field_lon(s):
            copy.wait_send()

    for w in range(len(waves)):
        wave_total(w).wait_send()
    for m in range(metas):
        meta_total(m).wait_send()


def shards(n_lon, n_lat, innovations, fractions, cell_index, counts, blocks, u_wind, v_wind, channel_mix):
    slots, devices, channels, width = innovations.shape
    lat_cells, lon_cells = u_wind.shape[1:]
    tiles = counts.shape[2]
    per_tile = width // tiles
    within = lax.broadcasted_iota(jnp.int32, (1, 1, tiles, per_tile), 3)
    live = within < counts[..., None]
    block = jnp.where(live, blocks[..., None], -1).reshape(slots, devices, width)
    places = jnp.stack([cell_index, block], axis=2).astype(jnp.bfloat16)
    meta = jnp.concatenate([fractions, places], axis=2)
    metas, waves = -(-slots // 4), 1 - (1 - slots) // WAVE
    meta = jnp.pad(meta[::-1], ((0, 4 * metas - slots), (0, 0), (0, 0), (0, 0)))
    meta = meta.reshape(metas, 4, devices, 4, width)
    meta = jnp.transpose(meta, (0, 2, 1, 3, 4)).reshape(metas, devices, 16, width)

    tall, wide = lat_cells + 2 * EDGE, 2 * lon_cells
    f32, bf16, dma = jnp.float32, jnp.bfloat16, pltpu.SemaphoreType.DMA
    vmem = pl.BlockSpec(memory_space=pltpu.VMEM)
    out = pl.pallas_call(
        functools.partial(kernel, n_lon, n_lat, slots, lat_cells, lon_cells),
        out_shape=jax.ShapeDtypeStruct((CH, lat_cells, lon_cells), f32),
        in_specs=[
            pl.BlockSpec(memory_space=pltpu.SMEM),
            pl.BlockSpec(memory_space=pl.ANY),
            pl.BlockSpec(memory_space=pl.ANY),
            vmem,
            vmem,
        ],
        out_specs=vmem,
        scratch_shapes=[
            pltpu.VMEM((slots, devices, channels, width), bf16),
            pltpu.VMEM((metas, devices, 16, width), bf16),
            pltpu.VMEM((slots, devices // GROUP, 8, GROUP * width), f32),
            pltpu.VMEM((TILE * TILE, CH * lat_cells * lon_cells // TILE**2), f32),
            pltpu.VMEM((slots, CH, tall, wide), f32),
            pltpu.VMEM((2 * LEV, tall, wide), f32),
            pltpu.VMEM((2, tall, lon_cells), f32),
            pltpu.VMEM((2, tall, lon_cells), f32),
            pltpu.VMEM((slots, 2, tall, lon_cells), f32),
            pltpu.VMEM((slots, 2, tall, lon_cells), f32),
            dma((2,)),
            dma((waves,)),
            dma((waves,)),
            dma((metas,)),
            dma((metas,)),
            dma((2,)),
            dma((2,)),
            dma((2,)),
            dma((2,)),
            dma((slots, 2)),
            dma((slots, 2)),
            dma((slots, 2)),
            dma((slots, 2)),
        ],
        compiler_params=pltpu.CompilerParams(
            collective_id=0, has_side_effects=True, vmem_limit_bytes=48 * 1024 * 1024
        ),
    )(channel_mix, innovations, meta, u_wind, v_wind)
    return out.reshape(VARS, LEV, lat_cells, lon_cells)


def solution(mesh):
    in_specs = (
        P(None, ("lon", "lat"), None, None),
        P(None, ("lon", "lat"), None, None),
        P(None, ("lon", "lat"), None),
        P(None, ("lon", "lat"), None),
        P(None, ("lon", "lat"), None),
        P(None, "lat", "lon"),
        P(None, "lat", "lon"),
        P(),
    )
    out_specs = P(None, None, "lat", "lon")
    body = functools.partial(shards, mesh.shape["lon"], mesh.shape["lat"])
    return jax.shard_map(body, mesh=mesh, in_specs=in_specs, out_specs=out_specs, check_vma=False)
```

```python
import functools

import jax
import jax.numpy as jnp
from jax import lax
from jax.experimental import pallas as pl
from jax.experimental.pallas import tpu as pltpu
from jax.sharding import PartitionSpec as P

VARS = 4
LEV = 4
CH = 16
TILE = 16
KAPPA = 0.125
EDGE = 8
GROUP = 16
SIDE = 4
WAVE = 2
MESH = pl.DeviceIdType.MESH


def kernel(
    n_lon, n_lat, slots, lat_cells, lon_cells,
    mix_ref, innov_ref, meta_ref, u_ref, v_ref, out_ref,
    got_innov, got_meta, rows_buf, acc, field, wind, wind_send, wind_got, lon_send, lon_got,
    own_sem, innov_send, innov_recv, meta_send, meta_recv,
    wlat_send, wlat_recv, wlon_send, wlon_recv, flat_send, flat_recv, flon_send, flon_recv,
):
    devices = n_lon * n_lat
    my_lon, my_lat = lax.axis_index("lon"), lax.axis_index("lat")
    me = my_lon * n_lat + my_lat
    width = got_innov.shape[-1]
    span = GROUP * width
    tall = lat_cells + 2 * EDGE
    low, high = EDGE, EDGE + lat_cells
    waves = [(slots - 1, slots)]
    while waves[-1][0] > 0:
        end = waves[-1][0]
        waves.append((max(end - WAVE, 0), end))
    metas = got_meta.shape[0]

    lat_up = (my_lon, (my_lat + 1) % n_lat)
    lat_down = (my_lon, (my_lat + n_lat - 1) % n_lat)
    lon_up = ((my_lon + 1) % n_lon, my_lat)
    lon_down = ((my_lon + n_lon - 1) % n_lon, my_lat)

    barrier = pltpu.get_barrier_semaphore()

    @pl.loop(1, devices)
    def _(k):
        to = (me + k) % devices
        pl.semaphore_signal(barrier, inc=1, device_id=(to // n_lat, to % n_lat), device_id_type=MESH)

    own_a = pltpu.make_async_copy(innov_ref.at[:, me], got_innov.at[:, 0], own_sem.at[0])
    own_b = pltpu.make_async_copy(meta_ref.at[:, me], got_meta.at[:, 0], own_sem.at[1])
    own_a.start()
    own_b.start()
    wind[0:LEV, low:high, 0:lon_cells] = 0.5 * u_ref[...]
    wind[LEV : 2 * LEV, low:high, 0:lon_cells] = 0.5 * v_ref[...]
    pl.semaphore_wait(barrier, devices - 1)

    def lat_pair(buffer, send, recv):
        down = pltpu.make_async_remote_copy(
            src_ref=buffer.at[:, low : low + EDGE, 0:lon_cells],
            dst_ref=buffer.at[:, high : high + EDGE, 0:lon_cells],
            send_sem=send.at[0], recv_sem=recv.at[0], device_id=lat_down, device_id_type=MESH,
        )
        up = pltpu.make_async_remote_copy(
            src_ref=buffer.at[:, high - EDGE : high, 0:lon_cells],
            dst_ref=buffer.at[:, 0:low, 0:lon_cells],
            send_sem=send.at[1], recv_sem=recv.at[1], device_id=lat_up, device_id_type=MESH,
        )
        return down, up

    def lon_pair(send_buf, got_buf, send, recv):
        down = pltpu.make_async_remote_copy(
            src_ref=send_buf.at[0], dst_ref=got_buf.at[0],
            send_sem=send.at[0], recv_sem=recv.at[0], device_id=lon_down, device_id_type=MESH,
        )
        up = pltpu.make_async_remote_copy(
            src_ref=send_buf.at[1], dst_ref=got_buf.at[1],
            send_sem=send.at[1], recv_sem=recv.at[1], device_id=lon_up, device_id_type=MESH,
        )
        return down, up

    lane = lax.broadcasted_iota(jnp.int32, (tall, lon_cells), 1)

    def pack(source, count, target):
        first = jnp.zeros((tall, lon_cells), jnp.float32)
        last = first
        for c in range(count):
            body = source[c, :, 0:lon_cells]
            here = (lane >= EDGE * c) & (lane < EDGE * (c + 1))
            a = body if c == 0 else pltpu.roll(body, EDGE * c, 1)
            shift = (EDGE * (c + 1)) % lon_cells
            b = body if shift == 0 else pltpu.roll(body, shift, 1)
            first = jnp.where(here, a, first)
            last = jnp.where(here, b, last)
        target[0] = first
        target[1] = last

    def unpack(got, count, target):
        after, before = got[0], got[1]
        for c in range(count):
            back = (lon_cells - EDGE * c) % lon_cells
            a = after if back == 0 else pltpu.roll(after, back, 1)
            shift = (lon_cells - EDGE - EDGE * c) % lon_cells
            b = before if shift == 0 else pltpu.roll(before, shift, 1)
            target[c, :, lon_cells : 2 * lon_cells] = jnp.where(lane < EDGE, a, b)

    def field_lat(s):
        return lat_pair(field.at[s], flat_send.at[s], flat_recv.at[s])

    def field_lon(s):
        return lon_pair(lon_send.at[s], lon_got.at[s], flon_send.at[s], flon_recv.at[s])

    def wave(w, k, to):
        first, end = waves[w]
        return pltpu.make_async_remote_copy(
            src_ref=innov_ref.at[first:end, to], dst_ref=got_innov.at[first:end, k],
            send_sem=innov_send.at[w], recv_sem=innov_recv.at[w],
            device_id=(to // n_lat, to % n_lat), device_id_type=MESH,
        )

    def wave_total(w):
        first, end = waves[w]
        whole = got_innov.at[first:end, 1:devices]
        return pltpu.make_async_remote_copy(
            src_ref=whole, dst_ref=whole,
            send_sem=innov_send.at[w], recv_sem=innov_recv.at[w], device_id=lat_up, device_id_type=MESH,
        )

    def meta_copy(m, k, to):
        return pltpu.make_async_remote_copy(
            src_ref=meta_ref.at[m, to], dst_ref=got_meta.at[m, k],
            send_sem=meta_send.at[m], recv_sem=meta_recv.at[m],
            device_id=(to // n_lat, to % n_lat), device_id_type=MESH,
        )

    def meta_total(m):
        whole = got_meta.at[m, 1:devices]
        return pltpu.make_async_remote_copy(
            src_ref=whole, dst_ref=whole,
            send_sem=meta_send.at[m], recv_sem=meta_recv.at[m], device_id=lat_up, device_id_type=MESH,
        )

    wind_lat = lat_pair(wind, wlat_send, wlat_recv)
    wind_lon = lon_pair(wind_send, wind_got, wlon_send, wlon_recv)
    for copy in wind_lat:
        copy.start()

    def send_wave(w):
        @pl.loop(1, devices)
        def _(k):
            to = (me + k) % devices
            if w == 0:
                meta_copy(0, k, to).start()
            if w == 2:
                for m in range(1, metas):
                    meta_copy(m, k, to).start()
            wave(w, k, to).start()

    send_wave(0)
    send_wave(1)
    send_wave(2)
    own_a.wait()
    own_b.wait()
    for copy in wind_lat:
        copy.wait()
    pack(wind, 2 * LEV, wind_send)
    for copy in wind_lon:
        copy.start()

    across = lon_cells // TILE
    tile_id = lax.broadcasted_iota(jnp.int32, (TILE, span), 0).astype(jnp.float32)
    lane_group = lax.broadcasted_iota(jnp.int32, (CH, lon_cells), 1) // TILE
    contract = (((1,), (1,)), ((), ()))
    row_at = lax.broadcasted_iota(jnp.int32, (tall, 2 * lon_cells), 0)
    first_row = jnp.where(my_lat == 0, low, 0)
    last_row = jnp.where(my_lat == n_lat - 1, high, tall)
    inside = (row_at >= first_row) & (row_at < last_row)

    def stepped(older, channels):
        below = field[older, 0]
        totals = [mix_ref[0, c] * below for c in channels]
        for d in range(1, CH):
            below = field[older, d]
            totals = [total + mix_ref[d, c] * below for c, total in zip(channels, totals)]
        level = channels[0] % LEV
        half_u, half_v = wind[level], wind[LEV + level]
        results = []
        for total in totals:
            total = jnp.where(inside, total, 0.0)
            eastward = half_u * total
            northward = half_v * total
            near = KAPPA * total
            results.append(
                (1.0 - 4.0 * KAPPA) * total
                + pltpu.roll(near + eastward, 2 * lon_cells - 1, 1)
                + pltpu.roll(near - eastward, 1, 1)
                + pltpu.roll(near + northward, tall - 1, 0)
                + pltpu.roll(near - northward, 1, 0)
            )
        return results

    def same_level(i):
        first = (i // LEV) * LEV * SIDE + i % LEV
        return [first + LEV * j for j in range(SIDE)]

    def take_meta(m):
        meta_total(m).wait_recv()

        @pl.loop(0, devices // GROUP)
        def _(g):
            for i in range(GROUP):
                numbers = got_meta[m, g * GROUP + i].astype(jnp.float32)
                for j in range(4):
                    s = slots - 1 - (4 * m + j)
                    if s >= 0:
                        rows_buf[s, g, 0:4, i * width : (i + 1) * width] = numbers[4 * j : 4 * j + 4]

    def gather_slot(s):
        acc[...] = jnp.zeros(acc.shape, jnp.float32)

        @pl.loop(0, devices // GROUP)
        def _(g):
            values = jnp.concatenate(
                [got_innov[s, g * GROUP + i] for i in range(GROUP)], axis=1
            ).astype(jnp.float32)
            frac_y, frac_x = rows_buf[s, g, 0:1], rows_buf[s, g, 1:2]
            cell, block = rows_buf[s, g, 2:3], rows_buf[s, g, 3:4]
            row = jnp.floor(cell * (1.0 / TILE))
            col = cell - TILE * row
            in_rows = jnp.where(tile_id == row, 1.0 - frac_y, jnp.where(tile_id == row + 1.0, frac_y, 0.0))
            in_cols = jnp.where(tile_id == col, 1.0 - frac_x, jnp.where(tile_id == col + 1.0, frac_x, 0.0))
            heads, tails = [], []
            for r in range(TILE):
                weight = in_rows[r : r + 1] * in_cols
                head = weight.astype(jnp.bfloat16)
                heads.append(head)
                tails.append((weight - head.astype(jnp.float32)).astype(jnp.bfloat16))
            weights = jnp.concatenate(heads + tails, axis=0)
            blocks = jnp.broadcast_to(block, (CH, span))
            placed = []
            for b in range(lat_cells // TILE * across):
                placed.append(jnp.where(blocks == float(b), values, 0.0).astype(jnp.bfloat16))
            placed = jnp.concatenate(placed, axis=0)
            both = lax.dot_general(weights, placed, contract, preferred_element_type=jnp.float32)
            acc[...] += both[: TILE * TILE] + both[TILE * TILE :]

        tiles = jnp.transpose(acc[...])
        strips = []
        for down in range(lat_cells // TILE):
            for half in range(TILE // across):
                x = []
                for i in range(across):
                    b = down * across + i
                    x.append(tiles[b * CH : (b + 1) * CH, half * lon_cells : (half + 1) * lon_cells])
                apart = 1
                while apart < across:
                    moved = list(x)
                    for i in range(across):
                        if i & apart == 0:
                            j = i + apart
                            moved[i] = jnp.where(lane_group & apart == 0, x[i], pltpu.roll(x[j], TILE * apart, 1))
                            moved[j] = jnp.where(
                                lane_group & apart == 0, pltpu.roll(x[i], lon_cells - TILE * apart, 1), x[j]
                            )
                    x = moved
                    apart *= 2
                strips += x
        whole = jnp.stack(strips, axis=0)
        field[s, :, low:high, 0:lon_cells] = jnp.swapaxes(whole, 0, 1)

    def settle(s):
        for copy in field_lon(s):
            copy.wait_recv()
        unpack(lon_got.at[s], CH, field.at[s])

        @pl.when(s < slots - 1)
        def _():
            @pl.loop(0, CH // SIDE)
            def _(i):
                channels = same_level(i)
                news = [new + field[s, c] for c, new in zip(channels, stepped(s + 1, channels))]
                for c, new in zip(channels, news):
                    field[s, c] = new

    @pl.loop(0, slots)
    def _(n):
        s = slots - 1 - n
        for w, (_, end) in enumerate(waves):

            @pl.when(s == end - 1)
            def _():
                wave_total(w).wait_recv()

        for m in range(metas):

            @pl.when(n == 4 * m)
            def _():
                take_meta(m)

        gather_slot(s)

        @pl.when(s > 0)
        def _():
            for copy in field_lat(s):
                copy.start()

        @pl.when(n >= 1)
        def _():
            for copy in field_lat(s + 1):
                copy.wait()
            pack(field.at[s + 1], CH, lon_send.at[s + 1])
            for copy in field_lon(s + 1):
                copy.start()

        for w in range(3, len(waves)):

            @pl.when(n == WAVE * w - 5)
            def _():
                send_wave(w)

        @pl.when(n == 1)
        def _():
            for copy in wind_lon:
                copy.wait()
            unpack(wind_got, 2 * LEV, wind)

        @pl.when(n >= 2)
        def _():
            settle(s + 2)

    settle(1)

    @pl.loop(0, CH // SIDE)
    def _(i):
        channels = same_level(i)
        for c, new in zip(channels, stepped(1, channels)):
            out_ref[c] = new[low:high, 0:lon_cells] + field[0, c, low:high, 0:lon_cells]

    @pl.loop(1, slots)
    def _(s):
        for copy in field_lon(s):
            copy.wait_send()

    for w in range(len(waves)):
        wave_total(w).wait_send()
    for m in range(metas):
        meta_total(m).wait_send()


def shards(n_lon, n_lat, innovations, fractions, cell_index, counts, blocks, u_wind, v_wind, channel_mix):
    slots, devices, channels, width = innovations.shape
    lat_cells, lon_cells = u_wind.shape[1:]
    tiles = counts.shape[2]
    per_tile = width // tiles
    within = lax.broadcasted_iota(jnp.int32, (1, 1, tiles, per_tile), 3)
    live = within < counts[..., None]
    block = jnp.where(live, blocks[..., None], -1).reshape(slots, devices, width)
    places = jnp.stack([cell_index, block], axis=2).astype(jnp.bfloat16)
    meta = jnp.concatenate([fractions, places], axis=2)
    metas, waves = -(-slots // 4), 1 - (1 - slots) // WAVE
    meta = jnp.pad(meta[::-1], ((0, 4 * metas - slots), (0, 0), (0, 0), (0, 0)))
    meta = meta.reshape(metas, 4, devices, 4, width)
    meta = jnp.transpose(meta, (0, 2, 1, 3, 4)).reshape(metas, devices, 16, width)

    tall, wide = lat_cells + 2 * EDGE, 2 * lon_cells
    f32, bf16, dma = jnp.float32, jnp.bfloat16, pltpu.SemaphoreType.DMA
    vmem = pl.BlockSpec(memory_space=pltpu.VMEM)
    out = pl.pallas_call(
        functools.partial(kernel, n_lon, n_lat, slots, lat_cells, lon_cells),
        out_shape=jax.ShapeDtypeStruct((CH, lat_cells, lon_cells), f32),
        in_specs=[
            pl.BlockSpec(memory_space=pltpu.SMEM),
            pl.BlockSpec(memory_space=pl.ANY),
            pl.BlockSpec(memory_space=pl.ANY),
            vmem,
            vmem,
        ],
        out_specs=vmem,
        scratch_shapes=[
            pltpu.VMEM((slots, devices, channels, width), bf16),
            pltpu.VMEM((metas, devices, 16, width), bf16),
            pltpu.VMEM((slots, devices // GROUP, 8, GROUP * width), f32),
            pltpu.VMEM((TILE * TILE, CH * lat_cells * lon_cells // TILE**2), f32),
            pltpu.VMEM((slots, CH, tall, wide), f32),
            pltpu.VMEM((2 * LEV, tall, wide), f32),
            pltpu.VMEM((2, tall, lon_cells), f32),
            pltpu.VMEM((2, tall, lon_cells), f32),
            pltpu.VMEM((slots, 2, tall, lon_cells), f32),
            pltpu.VMEM((slots, 2, tall, lon_cells), f32),
            dma((2,)),
            dma((waves,)),
            dma((waves,)),
            dma((metas,)),
            dma((metas,)),
            dma((2,)),
            dma((2,)),
            dma((2,)),
            dma((2,)),
            dma((slots, 2)),
            dma((slots, 2)),
            dma((slots, 2)),
            dma((slots, 2)),
        ],
        compiler_params=pltpu.CompilerParams(
            collective_id=0, has_side_effects=True, vmem_limit_bytes=48 * 1024 * 1024
        ),
    )(channel_mix, innovations, meta, u_wind, v_wind)
    return out.reshape(VARS, LEV, lat_cells, lon_cells)


def solution(mesh):
    in_specs = (
        P(None, ("lon", "lat"), None, None),
        P(None, ("lon", "lat"), None, None),
        P(None, ("lon", "lat"), None),
        P(None, ("lon", "lat"), None),
        P(None, ("lon", "lat"), None),
        P(None, "lat", "lon"),
        P(None, "lat", "lon"),
        P(),
    )
    out_specs = P(None, None, "lat", "lon")
    body = functools.partial(shards, mesh.shape["lon"], mesh.shape["lat"])
    return jax.shard_map(body, mesh=mesh, in_specs=in_specs, out_specs=out_specs, check_vma=False)
```
